256 devices in a mesh: rad: 4 (over y), az: 64 (over x, z, core).
Axes of the slice: x: 4, y: 4, z: 8, core: 2. Of those that a mesh axis runs over, the one named last changes fastest.
Arguments:
- fields: float32 [2, 1, 1024, 8192], P(None, None, 'rad', 'az'), may hold values from -6 to 6
- whole_shift: int32 [1024], P('rad'), may hold values from -2048 to 2047
- frac_shift: float32 [1024], P('rad'), may hold values from -0.5 to 0.5
- inv_spacing: float32 [1024], P('rad'), may hold values from 0.5 to 2
Outputs:
- remapped: float32 [2, 1, 1024, 8192], P(None, None, 'rad', 'az')
- radial_derivative: float32 [2, 1, 1024, 8192], P(None, None, 'rad', 'az')
The draws below stay inside these ranges and needn't reach their ends.
All inputs are finite; a program needn't handle non-finite values.
Results may differ from the reference program's by a relative error of at most 0.0001.
Values sent between devices are 32-bit elements; how exact they have to be, the bound alone decides.
No kernel may reach another device: no remote copies, remote signals or barrier semaphores. Data moves between devices by JAX's collectives and lax.ppermute only.
A program may use at most 256 MiB of HBM per device.

```python
import math
import jax
import jax.numpy as jnp
from jax import lax

FIELDS = 2
Z = 1
BLOCK = 128
NY = 8192
NX = 1024


def set_ends(drawn, own_key, least, high):
    shape = drawn.shape
    spot = [jax.random.randint(jax.random.fold_in(own_key, axis), (), 0, shape[axis]) for axis in range(len(shape))]
    drawn = drawn.at[tuple(spot)].set(least)
    longest = shape.index(max(shape))
    spot[longest] = (spot[longest] + 1) % shape[longest]
    return drawn.at[tuple(spot)].set(high)


def block_levels(stream_key, shape, split, least, top_value):
    level, own = 1.0, jax.random.fold_in(stream_key, 6)
    for dim, blocks in split:
        steps = jnp.exp(jax.random.uniform(jax.random.fold_in(own, dim), (blocks,), jnp.float32, least / len(split), top_value / len(split)))
        level = level * jnp.repeat(steps, shape[dim] // blocks).reshape([-1 if axis == dim else 1 for axis in range(len(shape))])
    return level


def gaussian(rng, extent, scale, limit, split=(), kind=jnp.bfloat16):
    array = scale * jax.random.normal(rng, extent, jnp.float32)
    if split:
        array = array * block_levels(rng, extent, split, -0.22, 0.18)
    return jnp.clip(array, -limit, limit).astype(kind)


def setup_inputs(seed: int = 0) -> dict:
    key_of = jax.random.split(jax.random.key(seed), 5)
    fields = gaussian(key_of[0], (FIELDS, Z, NX, NY), 1.0, 6.0, ((2, 4), (3, 64)), jnp.float32)
    whole_shift = set_ends(jax.random.randint(key_of[1], (NX,), 0 - NY // 4, NY // 4), jax.random.fold_in(key_of[1], 1), 0 - NY // 4, (NY // 4) - 1).astype(jnp.int32)
    frac_shift = jnp.clip(jax.random.uniform(key_of[2], (NX,), jnp.float32, -0.5, 0.5) * block_levels(key_of[2], (NX,), ((0, 4),), -0.4, 0.0), -0.5, 0.5)
    inv_spacing = jnp.clip(jnp.exp(math.log(2.0) - 1.3862944 * jax.random.uniform(key_of[3], (NX,), jnp.float32) ** block_levels(key_of[3], (NX,), ((0, 4),), -0.2, 0.2)), 0.5, 2.0)
    return dict(fields=fields, whole_shift=whole_shift, frac_shift=frac_shift, inv_spacing=inv_spacing)


HIGHEST = lax.Precision.HIGHEST


def compact_inverse(size):
    identity = jnp.eye(size, dtype=jnp.float32)
    offdiag = 0.25 * (jnp.eye(size, k=1, dtype=jnp.float32) + jnp.eye(size, k=-1, dtype=jnp.float32))
    inverse = identity - offdiag
    power = offdiag
    for square_step in range(5):
        power = jnp.dot(power, power, precision=HIGHEST)
        inverse = jnp.dot(inverse, identity + power, precision=HIGHEST)
    return inverse


def reference(fields, whole_shift, frac_shift, inv_spacing):
    spectrum = jnp.fft.fft(fields, axis=-1)
    wavenumber = jnp.arange(NY, dtype=jnp.int32)
    signed = jnp.where(wavenumber < NY // 2, wavenumber, wavenumber - NY)
    phase_turns = jnp.mod(signed[None, :] * whole_shift[:, None], NY).astype(jnp.float32)
    phase_turns = phase_turns + signed[None, :].astype(jnp.float32) * frac_shift[:, None]
    phase_angle = (2.0 * jnp.pi / NY) * phase_turns
    shifted = spectrum * (jnp.cos(phase_angle) - 1j * jnp.sin(phase_angle))
    remapped = jnp.real(jnp.fft.ifft(shifted, axis=-1)).astype(jnp.float32)
    padded = jnp.pad(remapped, ((0, 0), (0, 0), (1, 1), (0, 0)))
    right_side = 0.75 * (padded[:, :, 2:] - padded[:, :, :-2]) * inv_spacing[:, None]
    blocks = right_side.reshape(FIELDS, Z, NX // BLOCK, BLOCK, NY)
    radial_derivative = jnp.einsum("ab,fzgbl->fzgal", compact_inverse(BLOCK), blocks, precision=HIGHEST)
    return remapped, radial_derivative.reshape(FIELDS, Z, NX, NY)
```

```python
import math

import jax
import jax.numpy as jnp
import numpy as np
from jax import lax
from jax.experimental import pallas as pl
from jax.experimental.pallas import tpu as pltpu
from jax.sharding import PartitionSpec as P

BLOCK = 128


def compact_inverse(size):
    identity = np.eye(size)
    offdiag = 0.25 * (np.eye(size, k=1) + np.eye(size, k=-1))
    inverse = identity - offdiag
    power = offdiag
    for _ in range(5):
        power = power @ power
        inverse = inverse @ (identity + power)
    return inverse.astype(np.float32)


def halves(table):
    high = np.asarray(table, np.float32).astype(jnp.bfloat16)
    low = (np.asarray(table, np.float32) - high.astype(np.float32)).astype(jnp.bfloat16)
    return high, low


def split(value):
    high = value.astype(jnp.bfloat16)
    return high, (value - high.astype(jnp.float32)).astype(jnp.bfloat16)


def dot3(left, right):
    def dot(a, b):
        return jnp.dot(a, b, preferred_element_type=jnp.float32)

    return dot(left[0], right[0]) + (dot(left[0], right[1]) + dot(left[1], right[0]))


def tables(groups, width, rows):
    half = groups // 2
    low = np.arange(half + 1)
    group = np.arange(groups)
    column = np.arange(width)
    across = 2 * np.pi * (low[:, None] * group[None, :] % groups) / groups
    real_rows = np.cos(across)
    imag_rows = -np.sin(across)[1:half]
    forward = np.concatenate([real_rows, imag_rows])
    weight = np.where((low == 0) | (low == half), 1.0, 2.0)[:, None]
    inverse = np.concatenate([weight * real_rows, 2.0 * imag_rows]).T / (groups * width)
    same_row = np.eye(rows)
    forward = np.kron(forward, same_row)
    inverse = np.kron(inverse, same_row)
    grid = 2 * np.pi * (column[:, None] * column[None, :] % width) / width
    cosine, sine = np.cos(grid), np.sin(grid)
    along = np.block([[cosine, -sine], [sine, cosine]])
    back = np.block([[cosine, sine], [-sine, cosine]])
    twist = 2 * np.pi * low[:, None] * column[None, :] / (groups * width)
    twist = np.stack([np.cos(twist), np.sin(twist)]).astype(np.float32)
    return [*halves(forward), *halves(along), *halves(back), *halves(inverse), twist]


def row_values(ref, first, rows):
    shape = (rows, ref.shape[1])
    lane = lax.broadcasted_iota(jnp.int32, shape, 1)
    row = lax.broadcasted_iota(jnp.int32, shape, 0)
    picked = jnp.where(lane == first + row, jnp.broadcast_to(ref[...], shape), 0.0)
    return jnp.sum(picked, axis=1, keepdims=True)


def shear_kernel(
    position_ref,
    signal_ref,
    whole_ref,
    frac_ref,
    forward_high,
    forward_low,
    along_high,
    along_low,
    back_high,
    back_low,
    inverse_high,
    inverse_low,
    twist_ref,
    out_ref,
    spectrum_ref,
    signal_scratch,
):
    groups, rows, width = signal_ref.shape
    half = groups // 2
    total = groups * width
    row_count = whole_ref.shape[1]
    first = lax.rem(position_ref[0] * rows, row_count)
    whole = row_values(whole_ref, first, rows).astype(jnp.int32)
    frac = row_values(frac_ref, first, rows)

    column = lax.broadcasted_iota(jnp.int32, (rows, width), 1)
    signed = jnp.where(column < width // 2, column, column - width)
    turns = ((signed * whole) & (width - 1)).astype(jnp.float32) + signed.astype(jnp.float32) * frac
    angle = (2.0 * math.pi / width) * turns
    wide_cos, wide_sin = jnp.cos(angle), jnp.sin(angle)
    turns = ((column * whole) & (total - 1)).astype(jnp.float32) + column.astype(jnp.float32) * frac
    angle = (2.0 * math.pi / total) * turns
    fine_cos, fine_sin = jnp.cos(angle), jnp.sin(angle)

    signal = signal_ref[...].reshape(groups * rows, width)
    signal_scratch[...] = dot3((forward_high[...], forward_low[...]), split(signal))
    for k in range(half + 1):
        here = pl.ds(k * rows, rows)
        cosine, sine = twist_ref[0, pl.ds(k, 1), :], twist_ref[1, pl.ds(k, 1), :]
        real = signal_scratch[here, :]
        if 0 < k < half:
            imag = signal_scratch[pl.ds((half + k) * rows, rows), :]
            spectrum_ref[here, :width] = real * cosine + imag * sine
            spectrum_ref[here, width:] = imag * cosine - real * sine
        else:
            spectrum_ref[here, :width] = real * cosine
            spectrum_ref[here, width:] = -real * sine
    spectrum_ref[...] = dot3(split(spectrum_ref[...]), (along_high[...], along_low[...]))
    for k in range(half + 1):
        here = pl.ds(k * rows, rows)
        cosine, sine = fine_cos[:, k : k + 1], fine_sin[:, k : k + 1]
        shift_cos = wide_cos * cosine - wide_sin * sine
        shift_sin = wide_cos * sine + wide_sin * cosine
        real, imag = spectrum_ref[here, :width], spectrum_ref[here, width:]
        spectrum_ref[here, :width] = real * shift_cos + imag * shift_sin
        spectrum_ref[here, width:] = imag * shift_cos - real * shift_sin
    spectrum_ref[...] = dot3(split(spectrum_ref[...]), (back_high[...], back_low[...]))
    for k in range(half + 1):
        here = pl.ds(k * rows, rows)
        cosine, sine = twist_ref[0, pl.ds(k, 1), :], twist_ref[1, pl.ds(k, 1), :]
        real, imag = spectrum_ref[here, :width], spectrum_ref[here, width:]
        signal_scratch[here, :] = real * cosine - imag * sine
        if 0 < k < half:
            signal_scratch[pl.ds((half + k) * rows, rows), :] = real * sine + imag * cosine
    shifted = dot3((inverse_high[...], inverse_low[...]), split(signal_scratch[...]))
    out_ref[...] = shifted.reshape(groups, rows, width)


def shear(signal, whole, frac, position):
    groups, rows, width = signal.shape
    return pl.pallas_call(
        shear_kernel,
        out_shape=jax.ShapeDtypeStruct(signal.shape, jnp.float32),
        in_specs=[pl.BlockSpec(memory_space=pltpu.SMEM)] + [pl.BlockSpec(memory_space=pltpu.VMEM)] * 12,
        out_specs=pl.BlockSpec(memory_space=pltpu.VMEM),
        scratch_shapes=[
            pltpu.VMEM(((groups // 2 + 1) * rows, 2 * width), jnp.float32),
            pltpu.VMEM((groups * rows, width), jnp.float32),
        ],
        compiler_params=pltpu.CompilerParams(vmem_limit_bytes=32 * 2**20),
    )(position, signal, whole, frac, *[jnp.asarray(t) for t in tables(groups, width, rows)])


def derivative_kernel(remapped_ref, before_ref, after_ref, spacing_ref, compact_ref, out_ref):
    field_count, row_count, width = remapped_ref.shape
    scale = 0.75 * spacing_ref[...]
    row = lax.broadcasted_iota(jnp.int32, (row_count, width), 0)
    for field in range(field_count):
        cells = remapped_ref[field]
        above = jnp.where(row == 0, before_ref[field], pltpu.roll(cells, 1, 0))
        below = jnp.where(row == row_count - 1, after_ref[field], pltpu.roll(cells, row_count - 1, 0))
        difference = split(below - above)
        for start in range(0, row_count, BLOCK):
            here = slice(start, start + BLOCK)
            matrix = split(compact_ref[...] * scale[:, here])
            out_ref[field, here, :] = dot3(matrix, (difference[0][here], difference[1][here]))


def derivative(remapped, before, after, spacing):
    return pl.pallas_call(
        derivative_kernel,
        out_shape=jax.ShapeDtypeStruct(remapped.shape, jnp.float32),
        in_specs=[pl.BlockSpec(memory_space=pltpu.VMEM)] * 5,
        out_specs=pl.BlockSpec(memory_space=pltpu.VMEM),
        compiler_params=pltpu.CompilerParams(vmem_limit_bytes=32 * 2**20),
    )(remapped, before, after, spacing, jnp.asarray(compact_inverse(BLOCK)))


def on_device(fields, whole_shift, frac_shift, inv_spacing):
    groups = lax.axis_size("az")
    ends = lax.axis_size("rad") - 1
    position = lax.axis_index("az").astype(jnp.int32).reshape(1)
    field_count, plane_count, row_count, width = fields.shape
    sets = field_count * plane_count
    rows = sets * row_count // groups
    signal = fields.reshape(groups, rows, width)
    signal = lax.all_to_all(signal, "az", 0, 0, tiled=True)
    whole = whole_shift.astype(jnp.float32).reshape(1, row_count)
    signal = shear(signal, whole, frac_shift.reshape(1, row_count), position)
    signal = lax.all_to_all(signal, "az", 0, 0, tiled=True)
    remapped = signal.reshape(sets, row_count, width)
    before = lax.ppermute(remapped[:, -1:], "rad", [(i, i + 1) for i in range(ends)])
    after = lax.ppermute(remapped[:, :1], "rad", [(i + 1, i) for i in range(ends)])
    radial = derivative(remapped, before, after, inv_spacing.reshape(1, row_count))
    return remapped.reshape(fields.shape), radial.reshape(fields.shape)


def solution(mesh):
    return jax.shard_map(
        on_device,
        mesh=mesh,
        in_specs=(P(None, None, "rad", "az"), P("rad"), P("rad"), P("rad")),
        out_specs=(P(None, None, "rad", "az"), P(None, None, "rad", "az")),
        check_vma=False,
    )
```

```python
import functools
import math

import jax
import jax.numpy as jnp
import numpy as np
from jax import lax
from jax.experimental import pallas as pl
from jax.experimental.pallas import tpu as pltpu
from jax.sharding import PartitionSpec as P

BLOCK = 128
VMEM = pl.BlockSpec(memory_space=pltpu.VMEM)
SMEM = pl.BlockSpec(memory_space=pltpu.SMEM)
HBM = pl.BlockSpec(memory_space=pltpu.HBM)
PARAMS = pltpu.CompilerParams(vmem_limit_bytes=24 * 2**20)


def compact_inverse(size):
    identity = np.eye(size)
    offdiag = 0.25 * (np.eye(size, k=1) + np.eye(size, k=-1))
    inverse = identity - offdiag
    power = offdiag
    for _ in range(5):
        power = power @ power
        inverse = inverse @ (identity + power)
    return inverse.astype(np.float32)


def halves(table):
    high = np.asarray(table, np.float32).astype(jnp.bfloat16)
    low = (np.asarray(table, np.float32) - high.astype(np.float32)).astype(jnp.bfloat16)
    return high, low


def split(value):
    high = value.astype(jnp.bfloat16)
    return high, (value - high.astype(jnp.float32)).astype(jnp.bfloat16)


def dot(left, right):
    return jnp.dot(left, right, preferred_element_type=jnp.float32)


def dot3(left, right):
    return dot(left[0], right[0]) + (dot(left[0], right[1]) + dot(left[1], right[0]))


def fourier_tables(groups, width):
    half = groups // 2
    low = np.arange(half + 1)
    column = np.arange(width)
    across = 2 * np.pi * (low[:, None] * np.arange(groups)[None, :] % groups) / groups
    cosine, sine = np.cos(across), np.sin(across)
    forward = np.concatenate([cosine, -sine[1:half]])
    inverse = np.concatenate([cosine[:1], 2 * cosine[1:half], cosine[half:], -2 * sine[1:half]]).T / (groups * width)
    across = []
    for table in (forward, inverse):
        high, low = halves(table)
        across.append(np.pad(np.concatenate([high, high, low], axis=1), ((0, 0), (0, 2 * width - 3 * groups))))
    grid = 2 * np.pi * (column[:, None] * column[None, :] % width) / width
    cosine, sine = np.cos(grid), np.sin(grid)
    along = halves(np.block([[cosine, -sine], [sine, cosine]]))
    return np.concatenate([*across, *along])


def prepare_kernel(
    position_ref, whole_ref, frac_ref, spacing_ref, compact_ref, table_ref,
    table_out, twist_out, phase_out, matrix_out,
    *, groups, rows,
):
    table_out[...] = table_ref[...]
    scale = 0.75 * spacing_ref[...]
    for start in range(0, scale.shape[1], BLOCK):
        here = slice(start, start + BLOCK)
        matrix_out[:BLOCK, here], matrix_out[BLOCK:, here] = split(compact_ref[...] * scale[:, here])
    half = groups // 2
    width = twist_out.shape[2]
    total = groups * width
    row_count = whole_ref.shape[0]
    shape = (half, width)
    low = lax.broadcasted_iota(jnp.int32, shape, 0)
    column = lax.broadcasted_iota(jnp.int32, shape, 1)
    angle = (2.0 * math.pi / total) * (low * column).astype(jnp.float32)
    twist_out[0, :half, :] = jnp.cos(angle)
    twist_out[1, :half, :] = jnp.sin(angle)
    edge = lax.broadcasted_iota(jnp.int32, (rows, width), 1)
    angle = (2.0 * math.pi / total) * (half * edge).astype(jnp.float32)
    twist_out[0, half:, :] = jnp.cos(angle)
    twist_out[1, half:, :] = jnp.sin(angle)
    signed = low + groups * jnp.where(column < width // 2, column, column - width)
    edge = half + groups * jnp.where(edge < width // 2, edge, edge - width)
    edge_row = lax.broadcasted_iota(jnp.int32, (rows, width), 0)
    first = lax.rem(position_ref[0] * rows, row_count)
    edge_angle = jnp.zeros((rows, width), jnp.float32)
    for row in range(rows):
        whole, frac = whole_ref[first + row], frac_ref[first + row]
        turns = ((signed * whole) & (total - 1)).astype(jnp.float32) + signed.astype(jnp.float32) * frac
        angle = (2.0 * math.pi / total) * turns
        here = pl.ds(row * half, half)
        phase_out[0, here, :] = jnp.cos(angle)
        phase_out[1, here, :] = jnp.sin(angle)
        turns = ((edge * whole) & (total - 1)).astype(jnp.float32) + edge.astype(jnp.float32) * frac
        edge_angle = jnp.where(edge_row == row, (2.0 * math.pi / total) * turns, edge_angle)
    here = pl.ds(rows * half, rows)
    phase_out[0, here, :] = jnp.cos(edge_angle)
    phase_out[1, here, :] = jnp.sin(edge_angle)


def shear_kernel(signal_ref, phase_ref, table_ref, twist_ref, out_ref, edge_ref, *, groups):
    rows, width = edge_ref.shape
    half = groups // 2
    across, back = table_ref[:groups, : 3 * groups], table_ref[groups : 2 * groups, : 3 * groups]
    start = 2 * groups
    along_high = table_ref[start : start + 2 * width, :]
    along = jnp.concatenate([along_high, along_high, table_ref[start + 2 * width :, :]], axis=0)
    twist_cos, twist_sin = twist_ref[0, :half, :], twist_ref[1, :half, :]
    edge_cos, edge_sin = twist_ref[0, half:, :], twist_ref[1, half:, :]
    first = lax.broadcasted_iota(jnp.int32, (half, width), 0) == 0

    def stacked(blocks):
        high, low = split(jnp.concatenate(blocks, axis=1))
        return jnp.concatenate([high, low, high], axis=0)

    def transformed(value):
        high, low = split(value)
        return dot(jnp.concatenate([high, low, high], axis=1), along)

    signal = dot(across, stacked([signal_ref[pl.ds(row, groups, stride=rows), :] for row in range(rows)]))
    blocks = []
    for row in range(rows):
        here = slice(row * width, (row + 1) * width)
        real, imag = signal[:half, here], signal[half:, here]
        edge_ref[pl.ds(row, 1), :] = imag[:1, :]
        imag = jnp.where(first, 0.0, imag)
        blocks.append(
            jnp.concatenate([real * twist_cos + imag * twist_sin, imag * twist_cos - real * twist_sin], axis=1)
        )
    edge = edge_ref[...]
    edge = jnp.concatenate([edge * edge_cos, -edge * edge_sin], axis=1)
    spectrum = transformed(jnp.concatenate([*blocks, edge, jnp.zeros_like(edge)], axis=0))
    size = (half + 1) * rows
    shift_cos, shift_sin = phase_ref[0], phase_ref[1]
    real, imag = spectrum[:size, :width], spectrum[:size, width:]
    spectrum = jnp.concatenate([real * shift_cos + imag * shift_sin, real * shift_sin - imag * shift_cos], axis=1)
    spectrum = transformed(jnp.concatenate([spectrum, jnp.zeros_like(edge)], axis=0))
    edge = spectrum[half * rows : size, :]
    edge_ref[...] = edge[:, :width] * edge_cos + edge[:, width:] * edge_sin
    blocks = []
    for row in range(rows):
        here = slice(row * half, (row + 1) * half)
        real, imag = spectrum[here, :width], spectrum[here, width:]
        edge = jnp.broadcast_to(edge_ref[pl.ds(row, 1), :], (half, width))
        blocks.append(
            jnp.concatenate(
                [
                    real * twist_cos + imag * twist_sin,
                    jnp.where(first, edge, real * twist_sin - imag * twist_cos),
                ],
                axis=0,
            )
        )
    signal = dot(back, stacked(blocks))
    for row in range(rows):
        out_ref[pl.ds(row, groups, stride=rows), :] = signal[:, row * width : (row + 1) * width]


def derivative_kernel(
    block_ref, remapped_ref, before_ref, after_ref, matrix_ref, remapped_out, radial_out, radial, sems,
    *, blocks,
):
    field_count, row_count, width = remapped_ref.shape
    stores = [pltpu.make_async_copy(remapped_ref, remapped_out, sems.at[field_count])]
    stores[0].start()
    row = lax.broadcasted_iota(jnp.int32, (row_count, width), 0)
    parts = [slice(start, start + BLOCK) for start in range(0, row_count, BLOCK)]
    before = jnp.where(block_ref[0] > 0, before_ref[...], 0.0)
    after = jnp.where(block_ref[0] < blocks - 1, after_ref[...], 0.0)
    for field in range(field_count):
        cells = remapped_ref[field]
        above = jnp.where(row == 0, before[field : field + 1], pltpu.roll(cells, 1, 0))
        below = jnp.where(row == row_count - 1, after[field : field + 1], pltpu.roll(cells, row_count - 1, 0))
        high, low = split(below - above)
        for here in parts:
            matrix = (matrix_ref[:BLOCK, here], matrix_ref[BLOCK:, here])
            radial[field, here, :] = dot3(matrix, (high[here], low[here]))
        stores.append(pltpu.make_async_copy(radial.at[field], radial_out.at[field], sems.at[field]))
        stores[-1].start()
    for store in stores:
        store.wait()


def on_device(fields, whole_shift, frac_shift, inv_spacing):
    groups = lax.axis_size("az")
    blocks = lax.axis_size("rad")
    column = lax.axis_index("az").astype(jnp.int32).reshape(1)
    block = lax.axis_index("rad").astype(jnp.int32).reshape(1)
    field_count, plane_count, row_count, width = fields.shape
    sets = field_count * plane_count
    rows = sets * row_count // groups
    half = groups // 2
    table = fourier_tables(groups, width)
    float_of = functools.partial(jax.ShapeDtypeStruct, dtype=jnp.float32)

    signal = lax.all_to_all(fields.reshape(groups, rows, width), "az", 0, 0, tiled=True)
    table, twist, phases, matrix = pl.pallas_call(
        functools.partial(prepare_kernel, groups=groups, rows=rows),
        out_shape=(
            jax.ShapeDtypeStruct(table.shape, jnp.bfloat16),
            float_of((2, half + rows, width)),
            float_of((2, (half + 1) * rows, width)),
            jax.ShapeDtypeStruct((2 * BLOCK, row_count), jnp.bfloat16),
        ),
        in_specs=[SMEM] * 3 + [VMEM] * 3,
        out_specs=(VMEM,) * 4,
        compiler_params=PARAMS,
        cost_estimate=pl.CostEstimate(flops=10**9, transcendentals=10**5, bytes_accessed=2**21),
    )(
        column,
        whole_shift,
        frac_shift,
        inv_spacing.reshape(1, row_count),
        jnp.asarray(compact_inverse(BLOCK)),
        jnp.asarray(table),
    )
    signal = pl.pallas_call(
        functools.partial(shear_kernel, groups=groups),
        out_shape=float_of((groups * rows, width)),
        in_specs=[VMEM] * 4,
        out_specs=VMEM,
        scratch_shapes=[pltpu.VMEM((rows, width), jnp.float32)],
        compiler_params=PARAMS,
        cost_estimate=pl.CostEstimate(flops=10**9, transcendentals=0, bytes_accessed=2**21),
    )(signal.reshape(groups * rows, width), phases, table, twist)
    signal = lax.all_to_all(signal.reshape(groups, rows, width), "az", 0, 0, tiled=True)
    remapped = signal.reshape(sets, row_count, width)
    before = lax.ppermute(remapped[:, -1], "rad", [(i, (i + 1) % blocks) for i in range(blocks)])
    after = lax.ppermute(remapped[:, 0], "rad", [((i + 1) % blocks, i) for i in range(blocks)])
    remapped, radial = pl.pallas_call(
        functools.partial(derivative_kernel, blocks=blocks),
        out_shape=(float_of(remapped.shape), float_of(remapped.shape)),
        in_specs=[SMEM] + [VMEM] * 4,
        out_specs=(HBM, HBM),
        scratch_shapes=[pltpu.VMEM(remapped.shape, jnp.float32), pltpu.SemaphoreType.DMA((sets + 1,))],
        compiler_params=PARAMS,
    )(block, remapped, before, after, matrix)
    return remapped.reshape(fields.shape), radial.reshape(fields.shape)


def solution(mesh):
    return jax.shard_map(
        on_device,
        mesh=mesh,
        in_specs=(P(None, None, "rad", "az"), P("rad"), P("rad"), P("rad")),
        out_specs=(P(None, None, "rad", "az"), P(None, None, "rad", "az")),
        check_vma=False,
    )
```

```python
import functools
import math

import jax
import jax.numpy as jnp
import numpy as np
from jax import lax
from jax.experimental import pallas as pl
from jax.experimental.pallas import tpu as pltpu
from jax.sharding import PartitionSpec as P

BLOCK = 128
VMEM = pl.BlockSpec(memory_space=pltpu.VMEM)
SMEM = pl.BlockSpec(memory_space=pltpu.SMEM)
HBM = pl.BlockSpec(memory_space=pltpu.HBM)
PARAMS = pltpu.CompilerParams(vmem_limit_bytes=24 * 2**20)


def compact_inverse(size):
    identity = np.eye(size)
    offdiag = 0.25 * (np.eye(size, k=1) + np.eye(size, k=-1))
    inverse = identity - offdiag
    power = offdiag
    for _ in range(5):
        power = power @ power
        inverse = inverse @ (identity + power)
    return inverse.astype(np.float32)


def halves(table):
    high = np.asarray(table, np.float32).astype(jnp.bfloat16)
    low = (np.asarray(table, np.float32) - high.astype(np.float32)).astype(jnp.bfloat16)
    return high, low


def split(value):
    high = value.astype(jnp.bfloat16)
    return high, (value - high.astype(jnp.float32)).astype(jnp.bfloat16)


def dot(left, right):
    return jnp.dot(left, right, preferred_element_type=jnp.float32)


def dot3(left, right):
    return dot(left[0], right[0]) + (dot(left[0], right[1]) + dot(left[1], right[0]))


def fourier_tables(groups, width):
    half = groups // 2
    low = np.arange(half + 1)
    column = np.arange(width)
    across = 2 * np.pi * (low[:, None] * np.arange(groups)[None, :] % groups) / groups
    cosine, sine = np.cos(across), np.sin(across)
    forward = np.concatenate([cosine, -sine[1:half]])
    inverse = np.concatenate([cosine[:1], 2 * cosine[1:half], cosine[half:], -2 * sine[1:half]]).T / (groups * width)
    across = []
    for table in (forward, inverse):
        high, low = halves(table)
        across.append(np.pad(np.concatenate([high, high, low], axis=1), ((0, 0), (0, 2 * width - 3 * groups))))
    grid = 2 * np.pi * (column[:, None] * column[None, :] % width) / width
    cosine, sine = np.cos(grid), np.sin(grid)
    along = halves(np.block([[cosine, -sine], [sine, cosine]]))
    return np.concatenate([*across, *along])


def phase_angle(signed, whole, frac, total):
    turns = ((signed * whole) & (total - 1)).astype(jnp.float32) + signed.astype(jnp.float32) * frac
    return (2.0 * math.pi / total) * turns


def prepare_kernel(
    position_ref, whole_ref, frac_ref, spacing_ref, compact_ref, table_ref,
    table_out, twist_out, phase_out, matrix_out,
    *, groups, rows,
):
    table_out[...] = table_ref[...]
    scale = 0.75 * spacing_ref[...]
    for start in range(0, scale.shape[1], BLOCK):
        here = slice(start, start + BLOCK)
        matrix_out[:BLOCK, here], matrix_out[BLOCK:, here] = split(compact_ref[...] * scale[:, here])
    half = groups // 2
    width = twist_out.shape[2]
    total = groups * width
    row_count = whole_ref.shape[1]
    shape = (half, width)
    low = lax.broadcasted_iota(jnp.int32, shape, 0)
    column = lax.broadcasted_iota(jnp.int32, shape, 1)
    angle = (2.0 * math.pi / total) * (low * column).astype(jnp.float32)
    twist_out[0, :half, :] = jnp.cos(angle)
    twist_out[1, :half, :] = jnp.sin(angle)
    edge = lax.broadcasted_iota(jnp.int32, (rows, width), 1)
    angle = (2.0 * math.pi / total) * (half * edge).astype(jnp.float32)
    twist_out[0, half:, :] = jnp.cos(angle)
    twist_out[1, half:, :] = jnp.sin(angle)
    signed = low + groups * jnp.where(column < width // 2, column, column - width)
    edge = half + groups * jnp.where(edge < width // 2, edge, edge - width)
    edge_row = lax.broadcasted_iota(jnp.int32, (rows, width), 0)
    lane = lax.broadcasted_iota(jnp.int32, (rows, row_count), 1)
    first = lax.rem(position_ref[0] * rows, row_count)
    own = lane == first + lax.broadcasted_iota(jnp.int32, (rows, row_count), 0)
    wholes = jnp.sum(jnp.where(own, whole_ref[...].astype(jnp.float32), 0.0), axis=1, keepdims=True).astype(jnp.int32)
    fracs = jnp.sum(jnp.where(own, frac_ref[...], 0.0), axis=1, keepdims=True)
    edge_angle = jnp.zeros((rows, width), jnp.float32)
    for row in range(rows):
        whole, frac = wholes[row : row + 1], fracs[row : row + 1]
        angle = phase_angle(signed, whole, frac, total)
        here = pl.ds(row * half, half)
        phase_out[0, here, :] = jnp.cos(angle)
        phase_out[1, here, :] = jnp.sin(angle)
        edge_angle = jnp.where(edge_row == row, phase_angle(edge, whole, frac, total), edge_angle)
    here = pl.ds(rows * half, rows)
    phase_out[0, here, :] = jnp.cos(edge_angle)
    phase_out[1, here, :] = jnp.sin(edge_angle)


def sheared(signals, table_ref, twist_ref, shift_cos, shift_sin, edge_ref):
    groups, width = signals[0].shape
    half = groups // 2
    edges = edge_ref.shape[0]
    size = half * len(signals)
    across, back = table_ref[:groups, : 3 * groups], table_ref[groups : 2 * groups, : 3 * groups]
    start = 2 * groups
    along_high = table_ref[start : start + 2 * width, :]
    along = jnp.concatenate([along_high, along_high, table_ref[start + 2 * width :, :]], axis=0)
    twist_cos, twist_sin = twist_ref[0, :half, :], twist_ref[1, :half, :]
    edge_cos, edge_sin = twist_ref[0, half : half + 1, :], twist_ref[1, half : half + 1, :]
    first = lax.broadcasted_iota(jnp.int32, (half, width), 0) == 0

    def stacked(blocks):
        high, low = split(jnp.concatenate(blocks, axis=1))
        return jnp.concatenate([high, low, high], axis=0)

    def transformed(value):
        high, low = split(value)
        return dot(jnp.concatenate([high, low, high], axis=1), along)

    signal = dot(across, stacked(signals))
    blocks = []
    edge_ref[...] = jnp.zeros_like(edge_ref)
    for row in range(len(signals)):
        here = slice(row * width, (row + 1) * width)
        real, imag = signal[:half, here], signal[half:, here]
        edge_ref[pl.ds(row, 1), :] = imag[:1, :]
        imag = jnp.where(first, 0.0, imag)
        blocks.append(
            jnp.concatenate([real * twist_cos + imag * twist_sin, imag * twist_cos - real * twist_sin], axis=1)
        )
    edge = edge_ref[...]
    edge = jnp.concatenate([edge * edge_cos, -edge * edge_sin], axis=1)
    spectrum = transformed(jnp.concatenate([*blocks, edge], axis=0))
    real, imag = spectrum[:, :width], spectrum[:, width:]
    spectrum = jnp.concatenate([real * shift_cos + imag * shift_sin, real * shift_sin - imag * shift_cos], axis=1)
    spectrum = transformed(spectrum)
    edge = spectrum[size:, :]
    edge_ref[...] = edge[:, :width] * edge_cos + edge[:, width:] * edge_sin
    blocks = []
    for row in range(len(signals)):
        here = slice(row * half, (row + 1) * half)
        real, imag = spectrum[here, :width], spectrum[here, width:]
        edge = jnp.broadcast_to(edge_ref[pl.ds(row, 1), :], (half, width))
        parts = [real * twist_cos + imag * twist_sin, jnp.where(first, edge, real * twist_sin - imag * twist_cos)]
        blocks.append(jnp.concatenate(parts, axis=0))
    return dot(back, stacked(blocks))


def edge_kernel(block_ref, whole_ref, frac_ref, _, cells_ref, near_out, far_out, tiles, sems, *, blocks):
    sets, row_count, width = cells_ref.shape
    depth = tiles.shape[2]
    loads = []
    for side, start in enumerate((row_count - depth, 0)):
        for field in range(sets):
            source = cells_ref.at[field, pl.ds(start, depth)]
            loads.append(pltpu.make_async_copy(source, tiles.at[side, field], sems.at[side, field]))
            loads[-1].start()
    for load in loads:
        load.wait()
    edges = []
    for side, (row, place) in enumerate(((depth - 1, row_count - 1), (0, 0))):
        rows = [tiles[side, field, row : row + 1, :] for field in range(sets)]
        shifts = [whole_ref[:, place : place + 1].astype(jnp.float32), frac_ref[:, place : place + 1]]
        edges.append(jnp.concatenate(rows + [jnp.broadcast_to(shift, (1, width)) for shift in shifts], axis=0))
    is_odd = block_ref[0] & 1 == 1
    near_out[...] = jnp.where(is_odd, edges[1], edges[0])
    is_end = (block_ref[0] == 0) | (block_ref[0] == blocks - 1)
    far_out[...] = jnp.where(is_end, 0.0, jnp.where(is_odd, edges[0], edges[1]))


def halo_kernel(block_ref, near_ref, far_ref, phase_out, halo_out, *, groups, rows):
    is_odd = block_ref[0] & 1 == 1
    near, far = near_ref[...], far_ref[...]
    sides = (jnp.where(is_odd, near, far), jnp.where(is_odd, far, near))
    width = phase_out.shape[2]
    half = groups // 2
    shape = (half, width)
    sets = near_ref.shape[0] - 2
    low = lax.broadcasted_iota(jnp.int32, shape, 0)
    column = lax.broadcasted_iota(jnp.int32, shape, 1)
    signed = low + groups * jnp.where(column < width // 2, column, column - width)
    edge = lax.broadcasted_iota(jnp.int32, (rows, width), 1)
    edge = half + groups * jnp.where(edge < width // 2, edge, edge - width)
    edge_row = lax.broadcasted_iota(jnp.int32, (rows, width), 0)
    edge_angle = jnp.zeros((rows, width), jnp.float32)
    for side, cells in enumerate(sides):
        halo_out[pl.ds(side * sets, sets), :] = cells[:sets]
        whole, frac = cells[sets : sets + 1].astype(jnp.int32), cells[sets + 1 : sets + 2]
        angle = phase_angle(signed, whole, frac, groups * width)
        cosine, sine = jnp.cos(angle), jnp.sin(angle)
        for field in range(sets):
            here = pl.ds((side * sets + field) * half, half)
            phase_out[0, here, :] = cosine
            phase_out[1, here, :] = sine
        edge_angle = jnp.where(edge_row // sets == side, phase_angle(edge, whole, frac, groups * width), edge_angle)
    here = pl.ds(2 * sets * half, rows)
    phase_out[0, here, :] = jnp.cos(edge_angle)
    phase_out[1, here, :] = jnp.sin(edge_angle)


def shear_kernel(
    position_ref, signal_ref, phase_ref, halo_ref, halo_phase_ref, table_ref, twist_ref, out_ref, edge_ref,
    *, groups, rows,
):
    halos = halo_ref.shape[0]
    pitch = rows + halos
    half = groups // 2
    signals = [signal_ref[pl.ds(row, groups, stride=rows), :] for row in range(rows)]
    width = signals[0].shape[1]
    own = lax.broadcasted_iota(jnp.int32, (groups, width), 0) == position_ref[0]
    signals += [jnp.where(own, halo_ref[row : row + 1, :], 0.0) for row in range(halos)]
    shifts = []
    for part in range(2):
        ours, theirs = phase_ref[part], halo_phase_ref[part]
        cut, halo_cut = rows * half, halos * half
        shifts.append(jnp.concatenate([ours[:cut], theirs[:halo_cut], ours[cut:], theirs[halo_cut:]], axis=0))
    signal = sheared(signals, table_ref, twist_ref, *shifts, edge_ref)
    for row in range(pitch):
        out_ref[pl.ds(row, groups, stride=pitch), :] = signal[:, row * width : (row + 1) * width]


def derivative_kernel(
    cells_ref, matrix_ref, remapped_out, radial_out, remapped, radial, sems, *, groups, rows
):
    field_count, row_count, width = remapped.shape
    pitch = cells_ref.shape[0] // groups
    parts = row_count // rows
    for group in range(groups):
        here = pl.ds(group % parts * rows, rows)
        remapped[group // parts, here, :] = cells_ref[pl.ds(group * pitch, rows), :]
    stores = [pltpu.make_async_copy(remapped, remapped_out, sems.at[field_count])]
    stores[0].start()

    halos = [cells_ref[pl.ds(row, groups, stride=pitch), :] for row in range(rows, pitch)]
    halos = [jnp.sum(halo, axis=0, keepdims=True) for halo in halos]
    before, after = halos[:field_count], halos[field_count:]

    row = lax.broadcasted_iota(jnp.int32, (row_count, width), 0)
    for field in range(field_count):
        cells = remapped[field]
        above = jnp.where(row == 0, 0.0, pltpu.roll(cells, 1, 0))
        below = jnp.where(row == row_count - 1, 0.0, pltpu.roll(cells, row_count - 1, 0))
        high, low = split(below - above)
        for start in range(0, row_count, BLOCK):
            here = slice(start, start + BLOCK)
            matrix = (matrix_ref[:BLOCK, here], matrix_ref[BLOCK:, here])
            result = dot3(matrix, (high[here], low[here]))
            if start == 0:
                result -= (matrix[0][:, :1].astype(jnp.float32) + matrix[1][:, :1].astype(jnp.float32)) * before[field]
            if start == row_count - BLOCK:
                result += (matrix[0][:, -1:].astype(jnp.float32) + matrix[1][:, -1:].astype(jnp.float32)) * after[field]
            radial[field, here, :] = result
        stores.append(pltpu.make_async_copy(radial.at[field], radial_out.at[field], sems.at[field]))
        stores[-1].start()
    for store in stores:
        store.wait()


def on_device(fields, whole_shift, frac_shift, inv_spacing):
    groups = lax.axis_size("az")
    blocks = lax.axis_size("rad")
    column = lax.axis_index("az").astype(jnp.int32).reshape(1)
    block = lax.axis_index("rad").astype(jnp.int32).reshape(1)
    field_count, plane_count, row_count, width = fields.shape
    sets = field_count * plane_count
    rows = sets * row_count // groups
    half = groups // 2
    table = fourier_tables(groups, width)
    shifts = [row.reshape(1, row_count) for row in (whole_shift, frac_shift, inv_spacing)]
    float_of = functools.partial(jax.ShapeDtypeStruct, dtype=jnp.float32)

    signal = lax.all_to_all(fields.reshape(groups, rows, width), "az", 0, 0, tiled=True)
    table, twist, phases, matrix = pl.pallas_call(
        functools.partial(prepare_kernel, groups=groups, rows=rows),
        out_shape=(
            jax.ShapeDtypeStruct(table.shape, jnp.bfloat16),
            float_of((2, half + rows, width)),
            float_of((2, (half + 1) * rows, width)),
            jax.ShapeDtypeStruct((2 * BLOCK, row_count), jnp.bfloat16),
        ),
        in_specs=[SMEM] + [VMEM] * 5,
        out_specs=(VMEM,) * 4,
        compiler_params=PARAMS,
        cost_estimate=pl.CostEstimate(flops=10**9, transcendentals=10**5, bytes_accessed=2**21),
    )(
        column,
        *shifts,
        jnp.asarray(compact_inverse(BLOCK)),
        jnp.asarray(table),
    )
    planes = fields.reshape(sets, row_count, width)
    near, far = pl.pallas_call(
        functools.partial(edge_kernel, blocks=blocks),
        out_shape=(float_of((sets + 2, width)),) * 2,
        in_specs=[SMEM] + [VMEM] * 3 + [HBM],
        out_specs=(VMEM,) * 2,
        scratch_shapes=[pltpu.VMEM((2, sets, 8, width), jnp.float32), pltpu.SemaphoreType.DMA((2, sets))],
        compiler_params=PARAMS,
    )(block, *shifts, planes)
    near = lax.ppermute(near, "rad", [(i, i ^ 1) for i in range(blocks)])
    pairs = [(i, i + 1) for i in range(1, blocks - 1, 2)]
    far = lax.ppermute(far, "rad", pairs + [(j, i) for i, j in pairs] + [(0, blocks - 1), (blocks - 1, 0)])
    halo_phases, halo = pl.pallas_call(
        functools.partial(halo_kernel, groups=groups, rows=rows),
        out_shape=(float_of((2, 2 * sets * half + rows, width)), float_of((2 * sets, width))),
        in_specs=[SMEM] + [VMEM] * 2,
        out_specs=(VMEM,) * 2,
        compiler_params=PARAMS,
        cost_estimate=pl.CostEstimate(flops=10**8, transcendentals=10**4, bytes_accessed=2**18),
    )(block, near, far)
    pitch = rows + 2 * sets
    signal = pl.pallas_call(
        functools.partial(shear_kernel, groups=groups, rows=rows),
        out_shape=float_of((groups * pitch, width)),
        in_specs=[SMEM] + [VMEM] * 6,
        out_specs=VMEM,
        scratch_shapes=[pltpu.VMEM((2 * rows, width), jnp.float32)],
        compiler_params=PARAMS,
        cost_estimate=pl.CostEstimate(flops=10**9, transcendentals=0, bytes_accessed=2**21),
    )(column, signal.reshape(groups * rows, width), phases, halo, halo_phases, table, twist)
    signal = signal.reshape(groups, pitch // 4, 4, width)
    signal = lax.all_to_all(signal, "az", 0, 0, tiled=True).reshape(groups * pitch, width)
    whole_shape = (sets, row_count, width)
    remapped, radial = pl.pallas_call(
        functools.partial(derivative_kernel, groups=groups, rows=rows),
        out_shape=(float_of(whole_shape), float_of(whole_shape)),
        in_specs=[VMEM] * 2,
        out_specs=(HBM, HBM),
        scratch_shapes=[
            pltpu.VMEM(whole_shape, jnp.float32),
            pltpu.VMEM(whole_shape, jnp.float32),
            pltpu.SemaphoreType.DMA((sets + 1,)),
        ],
        compiler_params=PARAMS,
    )(signal, matrix)
    return remapped.reshape(fields.shape), radial.reshape(fields.shape)


def solution(mesh):
    return jax.shard_map(
        on_device,
        mesh=mesh,
        in_specs=(P(None, None, "rad", "az"), P("rad"), P("rad"), P("rad")),
        out_specs=(P(None, None, "rad", "az"), P(None, None, "rad", "az")),
        check_vma=False,
    )
```

```python
import functools
import math

import jax
import jax.numpy as jnp
import numpy as np
from jax import lax
from jax.experimental import pallas as pl
from jax.experimental.pallas import tpu as pltpu
from jax.sharding import PartitionSpec as P

BLOCK = 128
VMEM = pl.BlockSpec(memory_space=pltpu.VMEM)
SMEM = pl.BlockSpec(memory_space=pltpu.SMEM)
HBM = pl.BlockSpec(memory_space=pltpu.HBM)
PARAMS = pltpu.CompilerParams(vmem_limit_bytes=24 * 2**20)


def compact_inverse(size):
    identity = np.eye(size)
    offdiag = 0.25 * (np.eye(size, k=1) + np.eye(size, k=-1))
    inverse = identity - offdiag
    power = offdiag
    for _ in range(5):
        power = power @ power
        inverse = inverse @ (identity + power)
    return inverse.astype(np.float32)


def halves(table):
    high = np.asarray(table, np.float32).astype(jnp.bfloat16)
    low = (np.asarray(table, np.float32) - high.astype(np.float32)).astype(jnp.bfloat16)
    return high, low


def split(value):
    high = value.astype(jnp.bfloat16)
    return high, (value - high.astype(jnp.float32)).astype(jnp.bfloat16)


def dot(left, right):
    return jnp.dot(left, right, preferred_element_type=jnp.float32)


def dot3(left, right):
    return dot(left[0], right[0]) + (dot(left[0], right[1]) + dot(left[1], right[0]))


def fourier_tables(groups, width):
    half = groups // 2
    low = np.arange(half + 1)
    column = np.arange(width)
    across = 2 * np.pi * (low[:, None] * np.arange(groups)[None, :] % groups) / groups
    cosine, sine = np.cos(across), np.sin(across)
    forward = np.concatenate([cosine, -sine[1:half]])
    inverse = np.concatenate([cosine[:1], 2 * cosine[1:half], cosine[half:], -2 * sine[1:half]]).T / (groups * width)
    across = []
    for table in (forward, inverse):
        high, low = halves(table)
        across.append(np.pad(np.concatenate([high, high, low], axis=1), ((0, 0), (0, 2 * width - 3 * groups))))
    grid = 2 * np.pi * (column[:, None] * column[None, :] % width) / width
    cosine, sine = np.cos(grid), np.sin(grid)
    along = halves(np.block([[cosine, -sine], [sine, cosine]]))
    return np.concatenate([*across, *along])


def phase_angle(signed, whole, frac, total):
    turns = ((signed * whole) & (total - 1)).astype(jnp.float32) + signed.astype(jnp.float32) * frac
    return (2.0 * math.pi / total) * turns


def prepare_kernel(
    position_ref, whole_ref, frac_ref, spacing_ref, compact_ref, table_ref,
    table_out, twist_out, phase_out, matrix_out,
    *, groups, rows,
):
    table_out[...] = table_ref[...]
    scale = 0.75 * spacing_ref[...]
    for start in range(0, scale.shape[1], BLOCK):
        here = slice(start, start + BLOCK)
        matrix_out[:BLOCK, here], matrix_out[BLOCK:, here] = split(compact_ref[...] * scale[:, here])
    half = groups // 2
    width = twist_out.shape[2]
    total = groups * width
    row_count = whole_ref.shape[1]
    shape = (half, width)
    low = lax.broadcasted_iota(jnp.int32, shape, 0)
    column = lax.broadcasted_iota(jnp.int32, shape, 1)
    angle = (2.0 * math.pi / total) * (low * column).astype(jnp.float32)
    twist_out[0, :half, :] = jnp.cos(angle)
    twist_out[1, :half, :] = jnp.sin(angle)
    edge = lax.broadcasted_iota(jnp.int32, (rows, width), 1)
    angle = (2.0 * math.pi / total) * (half * edge).astype(jnp.float32)
    twist_out[0, half:, :] = jnp.cos(angle)
    twist_out[1, half:, :] = jnp.sin(angle)
    signed = low + groups * jnp.where(column < width // 2, column, column - width)
    edge = half + groups * jnp.where(edge < width // 2, edge, edge - width)
    edge_row = lax.broadcasted_iota(jnp.int32, (rows, width), 0)
    lane = lax.broadcasted_iota(jnp.int32, (rows, row_count), 1)
    first = lax.rem(position_ref[0] * rows, row_count)
    own = lane == first + lax.broadcasted_iota(jnp.int32, (rows, row_count), 0)
    wholes = jnp.sum(jnp.where(own, whole_ref[...].astype(jnp.float32), 0.0), axis=1, keepdims=True).astype(jnp.int32)
    fracs = jnp.sum(jnp.where(own, frac_ref[...], 0.0), axis=1, keepdims=True)
    edge_angle = jnp.zeros((rows, width), jnp.float32)
    for row in range(rows):
        whole, frac = wholes[row : row + 1], fracs[row : row + 1]
        angle = phase_angle(signed, whole, frac, total)
        here = pl.ds(row * half, half)
        phase_out[0, here, :] = jnp.cos(angle)
        phase_out[1, here, :] = jnp.sin(angle)
        edge_angle = jnp.where(edge_row == row, phase_angle(edge, whole, frac, total), edge_angle)
    here = pl.ds(rows * half, rows)
    phase_out[0, here, :] = jnp.cos(edge_angle)
    phase_out[1, here, :] = jnp.sin(edge_angle)


def sheared(signals, table_ref, twist_ref, shift_cos, shift_sin, edge_ref):
    groups, width = signals[0].shape
    half = groups // 2
    edges = edge_ref.shape[0]
    size = half * len(signals)
    across, back = table_ref[:groups, : 3 * groups], table_ref[groups : 2 * groups, : 3 * groups]
    start = 2 * groups
    along_high = table_ref[start : start + 2 * width, :]
    along = jnp.concatenate([along_high, along_high, table_ref[start + 2 * width :, :]], axis=0)
    twist_cos, twist_sin = twist_ref[0, :half, :], twist_ref[1, :half, :]
    edge_cos, edge_sin = twist_ref[0, half : half + 1, :], twist_ref[1, half : half + 1, :]
    first = lax.broadcasted_iota(jnp.int32, (half, width), 0) == 0

    def stacked(blocks):
        high, low = split(jnp.concatenate(blocks, axis=1))
        return jnp.concatenate([high, low, high], axis=0)

    def transformed(value):
        high, low = split(value)
        return dot(jnp.concatenate([high, low, high], axis=1), along)

    signal = dot(across, stacked(signals))
    blocks = []
    edge_ref[...] = jnp.zeros_like(edge_ref)
    for row in range(len(signals)):
        here = slice(row * width, (row + 1) * width)
        real, imag = signal[:half, here], signal[half:, here]
        edge_ref[pl.ds(row, 1), :] = imag[:1, :]
        imag = jnp.where(first, 0.0, imag)
        blocks.append(
            jnp.concatenate([real * twist_cos + imag * twist_sin, imag * twist_cos - real * twist_sin], axis=1)
        )
    edge = edge_ref[...]
    edge = jnp.concatenate([edge * edge_cos, -edge * edge_sin], axis=1)
    spectrum = transformed(jnp.concatenate([*blocks, edge], axis=0))
    real, imag = spectrum[:, :width], spectrum[:, width:]
    spectrum = jnp.concatenate([real * shift_cos + imag * shift_sin, real * shift_sin - imag * shift_cos], axis=1)
    spectrum = transformed(spectrum)
    edge = spectrum[size:, :]
    edge_ref[...] = edge[:, :width] * edge_cos + edge[:, width:] * edge_sin
    blocks = []
    for row in range(len(signals)):
        here = slice(row * half, (row + 1) * half)
        real, imag = spectrum[here, :width], spectrum[here, width:]
        edge = jnp.broadcast_to(edge_ref[pl.ds(row, 1), :], (half, width))
        parts = [real * twist_cos + imag * twist_sin, jnp.where(first, edge, real * twist_sin - imag * twist_cos)]
        blocks.append(jnp.concatenate(parts, axis=0))
    return dot(back, stacked(blocks))


def edge_kernel(position_ref, whole_ref, frac_ref, _, cells_ref, keep_out, give_out, tiles, sems):
    sets, row_count, width = cells_ref.shape
    depth = tiles.shape[2]
    loads = []
    for side, start in enumerate((row_count - depth, 0)):
        for field in range(sets):
            source = cells_ref.at[field, pl.ds(start, depth)]
            loads.append(pltpu.make_async_copy(source, tiles.at[side, field], sems.at[side, field]))
            loads[-1].start()
    for load in loads:
        load.wait()
    is_odd = position_ref[0] & 1 == 1
    last = [tiles[0, field, depth - 1 :, :] for field in range(sets)]
    first = [tiles[1, field, :1, :] for field in range(sets)]
    shifts = []
    for ref in (whole_ref, frac_ref):
        shift = jnp.where(is_odd, ref[:, :1].astype(jnp.float32), ref[:, row_count - 1 :].astype(jnp.float32))
        shifts.append(jnp.broadcast_to(shift, (1, width)))
    keep = [jnp.where(is_odd, theirs, ours) for ours, theirs in zip(last, first, strict=True)]
    keep_out[...] = jnp.concatenate(keep + shifts, axis=0)
    give_out[...] = jnp.concatenate([jnp.where(is_odd, ours, theirs) for ours, theirs in zip(last, first, strict=True)], axis=0)


def join_kernel(keep_ref, got_ref, out_ref):
    sets, _ = got_ref.shape
    out_ref[...] = jnp.zeros_like(out_ref)
    out_ref[pl.ds(0, sets + 2), :] = keep_ref[...]
    out_ref[pl.ds(sets + 2, sets), :] = got_ref[...]


def halo_kernel(position_ref, block_ref, edges_ref, phase_out, halo_out, *, groups, rows, blocks):
    is_odd = position_ref[0] & 1 == 1
    is_end = jnp.where(is_odd, block_ref[0] == blocks - 1, block_ref[0] == 0)
    cells = edges_ref[...]
    sets = halo_out.shape[0] // 2
    keep, got = cells[:sets], cells[sets + 2 : 2 * sets + 2]
    both = jnp.where(is_odd, jnp.concatenate([got, keep], axis=0), jnp.concatenate([keep, got], axis=0))
    halo_out[...] = jnp.where(is_end, 0.0, both)
    whole, frac = cells[sets : sets + 1].astype(jnp.int32), cells[sets + 1 : sets + 2]
    width = phase_out.shape[2]
    half = groups // 2
    shape = (half, width)
    low = lax.broadcasted_iota(jnp.int32, shape, 0)
    column = lax.broadcasted_iota(jnp.int32, shape, 1)
    signed = low + groups * jnp.where(column < width // 2, column, column - width)
    edge = lax.broadcasted_iota(jnp.int32, (rows, width), 1)
    edge = half + groups * jnp.where(edge < width // 2, edge, edge - width)
    angle, edge_angle = [phase_angle(place, whole, frac, groups * width) for place in (signed, edge)]
    for part, wave in enumerate((jnp.cos, jnp.sin)):
        shift = wave(angle)
        for field in range(sets):
            phase_out[part, pl.ds(field * half, half), :] = shift
        phase_out[part, pl.ds(sets * half, rows), :] = wave(edge_angle)


def shear_kernel(
    position_ref, signal_ref, phase_ref, halo_ref, halo_phase_ref, table_ref, twist_ref, out_ref, edge_ref,
    *, groups, rows,
):
    sets = halo_ref.shape[0] // 2
    pitch = rows + sets
    half = groups // 2
    signals = [signal_ref[pl.ds(row, groups, stride=rows), :] for row in range(rows)]
    width = signals[0].shape[1]
    group = lax.broadcasted_iota(jnp.int32, (groups, width), 0) - (position_ref[0] & -2)
    for field in range(sets):
        even, odd = halo_ref[field : field + 1, :], halo_ref[sets + field : sets + field + 1, :]
        signals.append(jnp.where(group == 0, even, jnp.where(group == 1, odd, 0.0)))
    shifts = []
    for part in range(2):
        ours, theirs = phase_ref[part], halo_phase_ref[part]
        cut, halo_cut = rows * half, sets * half
        shifts.append(jnp.concatenate([ours[:cut], theirs[:halo_cut], ours[cut:], theirs[halo_cut:]], axis=0))
    signal = sheared(signals, table_ref, twist_ref, *shifts, edge_ref)
    for row in range(pitch):
        out_ref[pl.ds(row, groups, stride=pitch), :] = signal[:, row * width : (row + 1) * width]


def derivative_kernel(
    cells_ref, matrix_ref, remapped_out, radial_out, remapped, radial, sems, *, groups, rows
):
    field_count, row_count, width = remapped.shape
    pitch = cells_ref.shape[0] // groups
    parts = row_count // rows
    for group in range(groups):
        here = pl.ds(group % parts * rows, rows)
        remapped[group // parts, here, :] = cells_ref[pl.ds(group * pitch, rows), :]
    stores = [pltpu.make_async_copy(remapped, remapped_out, sems.at[field_count])]
    stores[0].start()

    def total(place):
        return jnp.sum(cells_ref[pl.ds(place, groups // 2, stride=2 * pitch), :], axis=0, keepdims=True)

    before = [total(rows + field) for field in range(field_count)]
    after = [total(pitch + rows + field) for field in range(field_count)]

    row = lax.broadcasted_iota(jnp.int32, (row_count, width), 0)
    for field in range(field_count):
        cells = remapped[field]
        above = jnp.where(row == 0, 0.0, pltpu.roll(cells, 1, 0))
        below = jnp.where(row == row_count - 1, 0.0, pltpu.roll(cells, row_count - 1, 0))
        high, low = split(below - above)
        for start in range(0, row_count, BLOCK):
            here = slice(start, start + BLOCK)
            matrix = (matrix_ref[:BLOCK, here], matrix_ref[BLOCK:, here])
            result = dot3(matrix, (high[here], low[here]))
            if start == 0:
                result -= (matrix[0][:, :1].astype(jnp.float32) + matrix[1][:, :1].astype(jnp.float32)) * before[field]
            if start == row_count - BLOCK:
                result += (matrix[0][:, -1:].astype(jnp.float32) + matrix[1][:, -1:].astype(jnp.float32)) * after[field]
            radial[field, here, :] = result
        stores.append(pltpu.make_async_copy(radial.at[field], radial_out.at[field], sems.at[field]))
        stores[-1].start()
    for store in stores:
        store.wait()


def on_device(fields, whole_shift, frac_shift, inv_spacing):
    groups = lax.axis_size("az")
    blocks = lax.axis_size("rad")
    column = lax.axis_index("az").astype(jnp.int32).reshape(1)
    block = lax.axis_index("rad").astype(jnp.int32).reshape(1)
    field_count, plane_count, row_count, width = fields.shape
    sets = field_count * plane_count
    rows = sets * row_count // groups
    half = groups // 2
    table = fourier_tables(groups, width)
    shifts = [row.reshape(1, row_count) for row in (whole_shift, frac_shift, inv_spacing)]
    float_of = functools.partial(jax.ShapeDtypeStruct, dtype=jnp.float32)

    signal = lax.all_to_all(fields.reshape(groups, rows, width), "az", 0, 0, tiled=True)
    table, twist, phases, matrix = pl.pallas_call(
        functools.partial(prepare_kernel, groups=groups, rows=rows),
        out_shape=(
            jax.ShapeDtypeStruct(table.shape, jnp.bfloat16),
            float_of((2, half + rows, width)),
            float_of((2, (half + 1) * rows, width)),
            jax.ShapeDtypeStruct((2 * BLOCK, row_count), jnp.bfloat16),
        ),
        in_specs=[SMEM] + [VMEM] * 5,
        out_specs=(VMEM,) * 4,
        compiler_params=PARAMS,
        cost_estimate=pl.CostEstimate(flops=10**9, transcendentals=10**5, bytes_accessed=2**21),
    )(
        column,
        *shifts,
        jnp.asarray(compact_inverse(BLOCK)),
        jnp.asarray(table),
    )
    planes = fields.reshape(sets, row_count, width)
    keep, give = pl.pallas_call(
        edge_kernel,
        out_shape=(float_of((sets + 2, width)), float_of((sets, width))),
        in_specs=[SMEM] + [VMEM] * 3 + [HBM],
        out_specs=(VMEM,) * 2,
        scratch_shapes=[pltpu.VMEM((2, sets, 8, width), jnp.float32), pltpu.SemaphoreType.DMA((2, sets))],
        compiler_params=PARAMS,
    )(column, *shifts, planes)
    got = lax.ppermute(give, "az", [(i, i ^ 1) for i in range(groups)])
    edges = pl.pallas_call(
        join_kernel,
        out_shape=float_of((8, width)),
        in_specs=[VMEM] * 2,
        out_specs=VMEM,
        compiler_params=PARAMS,
    )(keep, got)
    pairs = [(i, j, (i + 1 - 2 * (j & 1)) % blocks) for i in range(blocks) for j in range(groups)]
    edges = lax.ppermute(edges, ("rad", "az"), [(i * groups + j, k * groups + j) for i, j, k in pairs])
    halo_phases, halo = pl.pallas_call(
        functools.partial(halo_kernel, groups=groups, rows=rows, blocks=blocks),
        out_shape=(float_of((2, sets * half + rows, width)), float_of((2 * sets, width))),
        in_specs=[SMEM] * 2 + [VMEM],
        out_specs=(VMEM,) * 2,
        compiler_params=PARAMS,
        cost_estimate=pl.CostEstimate(flops=10**8, transcendentals=10**4, bytes_accessed=2**18),
    )(column, block, edges)
    pitch = rows + sets
    signal = pl.pallas_call(
        functools.partial(shear_kernel, groups=groups, rows=rows),
        out_shape=float_of((groups * pitch, width)),
        in_specs=[SMEM] + [VMEM] * 6,
        out_specs=VMEM,
        scratch_shapes=[pltpu.VMEM((2 * rows, width), jnp.float32)],
        compiler_params=PARAMS,
        cost_estimate=pl.CostEstimate(flops=10**9, transcendentals=0, bytes_accessed=2**21),
    )(column, signal.reshape(groups * rows, width), phases, halo, halo_phases, table, twist)
    signal = signal.reshape(groups, pitch // 2, 2, width)
    signal = lax.all_to_all(signal, "az", 0, 0, tiled=True).reshape(groups * pitch, width)
    whole_shape = (sets, row_count, width)
    remapped, radial = pl.pallas_call(
        functools.partial(derivative_kernel, groups=groups, rows=rows),
        out_shape=(float_of(whole_shape), float_of(whole_shape)),
        in_specs=[VMEM] * 2,
        out_specs=(HBM, HBM),
        scratch_shapes=[
            pltpu.VMEM(whole_shape, jnp.float32),
            pltpu.VMEM(whole_shape, jnp.float32),
            pltpu.SemaphoreType.DMA((sets + 1,)),
        ],
        compiler_params=PARAMS,
    )(signal, matrix)
    return remapped.reshape(fields.shape), radial.reshape(fields.shape)


def solution(mesh):
    return jax.shard_map(
        on_device,
        mesh=mesh,
        in_specs=(P(None, None, "rad", "az"), P("rad"), P("rad"), P("rad")),
        out_specs=(P(None, None, "rad", "az"), P(None, None, "rad", "az")),
        check_vma=False,
    )
```

```python
import functools
import math

import jax
import jax.numpy as jnp
import numpy as np
from jax import lax
from jax.experimental import pallas as pl
from jax.experimental.pallas import tpu as pltpu
from jax.sharding import PartitionSpec as P

BLOCK = 128
THERE = (41, 59)
BACK = (41, 47)
VMEM = pl.BlockSpec(memory_space=pltpu.VMEM)
SMEM = pl.BlockSpec(memory_space=pltpu.SMEM)
HBM = pl.BlockSpec(memory_space=pltpu.HBM)
PARAMS = pltpu.CompilerParams(vmem_limit_bytes=24 * 2**20)


def compact_inverse(size):
    identity = np.eye(size)
    offdiag = 0.25 * (np.eye(size, k=1) + np.eye(size, k=-1))
    inverse = identity - offdiag
    power = offdiag
    for _ in range(5):
        power = power @ power
        inverse = inverse @ (identity + power)
    return inverse.astype(np.float32)


def halves(table):
    high = np.asarray(table, np.float32).astype(jnp.bfloat16)
    low = (np.asarray(table, np.float32) - high.astype(np.float32)).astype(jnp.bfloat16)
    return high, low


def split(value):
    high = value.astype(jnp.bfloat16)
    return high, (value - high.astype(jnp.float32)).astype(jnp.bfloat16)


def dot(left, right):
    return jnp.dot(left, right, preferred_element_type=jnp.float32)


def dot3(left, right):
    return dot(left[0], right[0]) + (dot(left[0], right[1]) + dot(left[1], right[0]))


def listed(order, groups):
    first, step = order
    return [(first + step * place) % groups for place in range(groups)]


def fourier_tables(groups, width):
    half = groups // 2
    low = np.arange(half + 1)
    column = np.arange(width)
    across = 2 * np.pi * (low[:, None] * np.arange(groups)[None, :] % groups) / groups
    cosine, sine = np.cos(across), np.sin(across)
    forward = np.concatenate([cosine, -sine[1:half]])
    inverse = np.concatenate([cosine[:1], 2 * cosine[1:half], cosine[half:], -2 * sine[1:half]]).T / (groups * width)
    across = []
    for table in (forward[:, listed(THERE, groups)], inverse[listed(BACK, groups)]):
        high, low = halves(table)
        across.append(np.pad(np.concatenate([high, high, low], axis=1), ((0, 0), (0, 2 * width - 3 * groups))))
    grid = 2 * np.pi * (column[:, None] * column[None, :] % width) / width
    cosine, sine = np.cos(grid), np.sin(grid)
    along = halves(np.block([[cosine, -sine], [sine, cosine]]))
    return np.concatenate([*across, *along])


def phase_angle(signed, whole, frac, total):
    turns = ((signed * whole) & (total - 1)).astype(jnp.float32) + signed.astype(jnp.float32) * frac
    return (2.0 * math.pi / total) * turns


def prepare_kernel(
    part_ref, whole_ref, frac_ref, spacing_ref, compact_ref, table_ref,
    table_out, twist_out, phase_out, matrix_out,
    *, groups, rows,
):
    table_out[...] = table_ref[...]
    scale = 0.75 * spacing_ref[...]
    for start in range(0, scale.shape[1], BLOCK):
        here = slice(start, start + BLOCK)
        matrix_out[:BLOCK, here], matrix_out[BLOCK:, here] = split(compact_ref[...] * scale[:, here])
    half = groups // 2
    width = twist_out.shape[2]
    total = groups * width
    row_count = whole_ref.shape[1]
    shape = (half, width)
    low = lax.broadcasted_iota(jnp.int32, shape, 0)
    column = lax.broadcasted_iota(jnp.int32, shape, 1)
    angle = (2.0 * math.pi / total) * (low * column).astype(jnp.float32)
    twist_out[0, :half, :] = jnp.cos(angle)
    twist_out[1, :half, :] = jnp.sin(angle)
    edge = lax.broadcasted_iota(jnp.int32, (rows, width), 1)
    angle = (2.0 * math.pi / total) * (half * edge).astype(jnp.float32)
    twist_out[0, half:, :] = jnp.cos(angle)
    twist_out[1, half:, :] = jnp.sin(angle)
    signed = low + groups * jnp.where(column < width // 2, column, column - width)
    edge = half + groups * jnp.where(edge < width // 2, edge, edge - width)
    edge_row = lax.broadcasted_iota(jnp.int32, (rows, width), 0)
    lane = lax.broadcasted_iota(jnp.int32, (rows, row_count), 1)
    first = lax.rem(part_ref[0] * rows, row_count)
    own = lane == first + lax.broadcasted_iota(jnp.int32, (rows, row_count), 0)
    wholes = jnp.sum(jnp.where(own, whole_ref[...].astype(jnp.float32), 0.0), axis=1, keepdims=True).astype(jnp.int32)
    fracs = jnp.sum(jnp.where(own, frac_ref[...], 0.0), axis=1, keepdims=True)
    edge_angle = jnp.zeros((rows, width), jnp.float32)
    for row in range(rows):
        whole, frac = wholes[row : row + 1], fracs[row : row + 1]
        angle = phase_angle(signed, whole, frac, total)
        here = pl.ds(row * half, half)
        phase_out[0, here, :] = jnp.cos(angle)
        phase_out[1, here, :] = jnp.sin(angle)
        edge_angle = jnp.where(edge_row == row, phase_angle(edge, whole, frac, total), edge_angle)
    here = pl.ds(rows * half, rows)
    phase_out[0, here, :] = jnp.cos(edge_angle)
    phase_out[1, here, :] = jnp.sin(edge_angle)


def sheared(signals, table_ref, twist_ref, shift_cos, shift_sin, edge_ref):
    groups, width = signals[0].shape
    half = groups // 2
    edges = edge_ref.shape[0]
    size = half * len(signals)
    across, back = table_ref[:groups, : 3 * groups], table_ref[groups : 2 * groups, : 3 * groups]
    start = 2 * groups
    along_high = table_ref[start : start + 2 * width, :]
    along = jnp.concatenate([along_high, along_high, table_ref[start + 2 * width :, :]], axis=0)
    twist_cos, twist_sin = twist_ref[0, :half, :], twist_ref[1, :half, :]
    edge_cos, edge_sin = twist_ref[0, half : half + 1, :], twist_ref[1, half : half + 1, :]
    first = lax.broadcasted_iota(jnp.int32, (half, width), 0) == 0

    def stacked(blocks):
        high, low = split(jnp.concatenate(blocks, axis=1))
        return jnp.concatenate([high, low, high], axis=0)

    def transformed(value):
        high, low = split(value)
        return dot(jnp.concatenate([high, low, high], axis=1), along)

    signal = dot(across, stacked(signals))
    blocks = []
    edge_ref[...] = jnp.zeros_like(edge_ref)
    for row in range(len(signals)):
        here = slice(row * width, (row + 1) * width)
        real, imag = signal[:half, here], signal[half:, here]
        edge_ref[pl.ds(row, 1), :] = imag[:1, :]
        imag = jnp.where(first, 0.0, imag)
        blocks.append(
            jnp.concatenate([real * twist_cos + imag * twist_sin, imag * twist_cos - real * twist_sin], axis=1)
        )
    edge = edge_ref[...]
    edge = jnp.concatenate([edge * edge_cos, -edge * edge_sin], axis=1)
    spectrum = transformed(jnp.concatenate([*blocks, edge], axis=0))
    real, imag = spectrum[:, :width], spectrum[:, width:]
    spectrum = jnp.concatenate([real * shift_cos + imag * shift_sin, real * shift_sin - imag * shift_cos], axis=1)
    spectrum = transformed(spectrum)
    edge = spectrum[size:, :]
    edge_ref[...] = edge[:, :width] * edge_cos + edge[:, width:] * edge_sin
    blocks = []
    for row in range(len(signals)):
        here = slice(row * half, (row + 1) * half)
        real, imag = spectrum[here, :width], spectrum[here, width:]
        edge = jnp.broadcast_to(edge_ref[pl.ds(row, 1), :], (half, width))
        parts = [real * twist_cos + imag * twist_sin, jnp.where(first, edge, real * twist_sin - imag * twist_cos)]
        blocks.append(jnp.concatenate(parts, axis=0))
    return dot(back, stacked(blocks))


def edge_kernel(position_ref, cells_ref, keep_out, give_out, tiles, sems):
    sets, row_count, width = cells_ref.shape
    depth = tiles.shape[2]
    loads = []
    for side, start in enumerate((row_count - depth, 0)):
        for field in range(sets):
            source = cells_ref.at[field, pl.ds(start, depth)]
            loads.append(pltpu.make_async_copy(source, tiles.at[side, field], sems.at[side, field]))
            loads[-1].start()
    for load in loads:
        load.wait()
    is_odd = position_ref[0] & 1 == 1
    last = [tiles[0, field, depth - 1 :, :] for field in range(sets)]
    first = [tiles[1, field, :1, :] for field in range(sets)]
    keep = [jnp.where(is_odd, theirs, ours) for ours, theirs in zip(last, first, strict=True)]
    keep_out[...] = jnp.concatenate(keep, axis=0)
    give_out[...] = jnp.concatenate([jnp.where(is_odd, ours, theirs) for ours, theirs in zip(last, first, strict=True)], axis=0)


def join_kernel(position_ref, whole_ref, frac_ref, _, keep_ref, got_ref, out_ref):
    sets, width = keep_ref.shape
    is_odd = position_ref[0] & 1 == 1
    last = whole_ref.shape[1] - 1
    out_ref[...] = jnp.zeros_like(out_ref)
    out_ref[pl.ds(0, sets), :] = keep_ref[...]
    out_ref[pl.ds(sets, sets), :] = got_ref[...]
    for place, ref in enumerate((whole_ref, frac_ref)):
        shift = jnp.where(is_odd, ref[:, :1].astype(jnp.float32), ref[:, last:].astype(jnp.float32))
        out_ref[pl.ds(2 * sets + place, 1), :] = jnp.broadcast_to(shift, (1, width))


def halo_kernel(position_ref, block_ref, edges_ref, phase_out, halo_out, *, groups, rows, blocks):
    is_odd = position_ref[0] & 1 == 1
    is_end = jnp.where(is_odd, block_ref[0] == blocks - 1, block_ref[0] == 0)
    cells = edges_ref[...]
    sets = halo_out.shape[0] // 2
    keep, got = cells[:sets], cells[sets : 2 * sets]
    both = jnp.where(is_odd, jnp.concatenate([got, keep], axis=0), jnp.concatenate([keep, got], axis=0))
    halo_out[...] = jnp.where(is_end, 0.0, both)
    whole, frac = cells[2 * sets : 2 * sets + 1].astype(jnp.int32), cells[2 * sets + 1 : 2 * sets + 2]
    width = phase_out.shape[2]
    half = groups // 2
    shape = (half, width)
    low = lax.broadcasted_iota(jnp.int32, shape, 0)
    column = lax.broadcasted_iota(jnp.int32, shape, 1)
    signed = low + groups * jnp.where(column < width // 2, column, column - width)
    edge = lax.broadcasted_iota(jnp.int32, (rows, width), 1)
    edge = half + groups * jnp.where(edge < width // 2, edge, edge - width)
    angle, edge_angle = [phase_angle(place, whole, frac, groups * width) for place in (signed, edge)]
    for part, wave in enumerate((jnp.cos, jnp.sin)):
        shift = wave(angle)
        for field in range(sets):
            phase_out[part, pl.ds(field * half, half), :] = shift
        phase_out[part, pl.ds(sets * half, rows), :] = wave(edge_angle)


def shear_kernel(
    position_ref, signal_ref, phase_ref, halo_ref, halo_phase_ref, table_ref, twist_ref, out_ref, edge_ref,
    *, groups, rows,
):
    sets = halo_ref.shape[0] // 2
    pitch = rows + sets
    half = groups // 2
    signals = [signal_ref[pl.ds(row, groups, stride=rows), :] for row in range(rows)]
    width = signals[0].shape[1]
    first, step = THERE
    group = (first + step * lax.broadcasted_iota(jnp.int32, (groups, width), 0)) & (groups - 1)
    group -= position_ref[0] & -2
    for field in range(sets):
        even, odd = halo_ref[field : field + 1, :], halo_ref[sets + field : sets + field + 1, :]
        signals.append(jnp.where(group == 0, even, jnp.where(group == 1, odd, 0.0)))
    shifts = []
    for part in range(2):
        ours, theirs = phase_ref[part], halo_phase_ref[part]
        cut, halo_cut = rows * half, sets * half
        shifts.append(jnp.concatenate([ours[:cut], theirs[:halo_cut], ours[cut:], theirs[halo_cut:]], axis=0))
    signal = sheared(signals, table_ref, twist_ref, *shifts, edge_ref)
    for row in range(pitch):
        out_ref[pl.ds(row, groups, stride=pitch), :] = signal[:, row * width : (row + 1) * width]


def derivative_kernel(
    cells_ref, matrix_ref, remapped_out, radial_out, remapped, radial, sems, *, groups, rows
):
    field_count, row_count, width = remapped.shape
    pitch = cells_ref.shape[0] // groups
    parts = row_count // rows
    there, back = listed(THERE, groups), listed(BACK, groups)
    for place, group in enumerate(back):
        part = there.index(group)
        here = pl.ds(part % parts * rows, rows)
        remapped[part // parts, here, :] = cells_ref[pl.ds(place * pitch, rows), :]
    stores = [pltpu.make_async_copy(remapped, remapped_out, sems.at[field_count])]
    stores[0].start()

    def total(place):
        return jnp.sum(cells_ref[pl.ds(place, groups // 2, stride=2 * pitch), :], axis=0, keepdims=True)

    before = [total(back[0] % 2 * pitch + rows + field) for field in range(field_count)]
    after = [total((1 - back[0] % 2) * pitch + rows + field) for field in range(field_count)]

    row = lax.broadcasted_iota(jnp.int32, (row_count, width), 0)
    for field in range(field_count):
        cells = remapped[field]
        above = jnp.where(row == 0, 0.0, pltpu.roll(cells, 1, 0))
        below = jnp.where(row == row_count - 1, 0.0, pltpu.roll(cells, row_count - 1, 0))
        high, low = split(below - above)
        for start in range(0, row_count, BLOCK):
            here = slice(start, start + BLOCK)
            matrix = (matrix_ref[:BLOCK, here], matrix_ref[BLOCK:, here])
            result = dot3(matrix, (high[here], low[here]))
            if start == 0:
                result -= (matrix[0][:, :1].astype(jnp.float32) + matrix[1][:, :1].astype(jnp.float32)) * before[field]
            if start == row_count - BLOCK:
                result += (matrix[0][:, -1:].astype(jnp.float32) + matrix[1][:, -1:].astype(jnp.float32)) * after[field]
            radial[field, here, :] = result
        stores.append(pltpu.make_async_copy(radial.at[field], radial_out.at[field], sems.at[field]))
        stores[-1].start()
    for store in stores:
        store.wait()


def on_device(fields, whole_shift, frac_shift, inv_spacing):
    groups = lax.axis_size("az")
    blocks = lax.axis_size("rad")
    column = lax.axis_index("az").astype(jnp.int32).reshape(1)
    part = (column - THERE[0]) * pow(THERE[1], -1, groups) & (groups - 1)
    block = lax.axis_index("rad").astype(jnp.int32).reshape(1)
    field_count, plane_count, row_count, width = fields.shape
    sets = field_count * plane_count
    rows = sets * row_count // groups
    half = groups // 2
    table = fourier_tables(groups, width)
    shifts = [row.reshape(1, row_count) for row in (whole_shift, frac_shift, inv_spacing)]
    float_of = functools.partial(jax.ShapeDtypeStruct, dtype=jnp.float32)

    signal = lax.all_to_all(
        fields.reshape(groups, rows, width), "az", 0, 0, axis_index_groups=[listed(THERE, groups)], tiled=True
    )
    table, twist, phases, matrix = pl.pallas_call(
        functools.partial(prepare_kernel, groups=groups, rows=rows),
        out_shape=(
            jax.ShapeDtypeStruct(table.shape, jnp.bfloat16),
            float_of((2, half + rows, width)),
            float_of((2, (half + 1) * rows, width)),
            jax.ShapeDtypeStruct((2 * BLOCK, row_count), jnp.bfloat16),
        ),
        in_specs=[SMEM] + [VMEM] * 5,
        out_specs=(VMEM,) * 4,
        compiler_params=PARAMS,
        cost_estimate=pl.CostEstimate(flops=10**9, transcendentals=10**5, bytes_accessed=2**21),
    )(
        part,
        *shifts,
        jnp.asarray(compact_inverse(BLOCK)),
        jnp.asarray(table),
    )
    planes = fields.reshape(sets, row_count, width)
    keep, give = pl.pallas_call(
        edge_kernel,
        out_shape=(float_of((sets, width)),) * 2,
        in_specs=[SMEM, HBM],
        out_specs=(VMEM,) * 2,
        scratch_shapes=[pltpu.VMEM((2, sets, 8, width), jnp.float32), pltpu.SemaphoreType.DMA((2, sets))],
        compiler_params=PARAMS,
    )(column, planes)
    got = lax.ppermute(give, "az", [(i, i ^ 1) for i in range(groups)])
    edges = pl.pallas_call(
        join_kernel,
        out_shape=float_of((8, width)),
        in_specs=[SMEM] + [VMEM] * 5,
        out_specs=VMEM,
        compiler_params=PARAMS,
    )(column, *shifts, keep, got)
    pairs = [(i, j, (i + 1 - 2 * (j & 1)) % blocks) for i in range(blocks) for j in range(groups)]
    edges = lax.ppermute(edges, ("rad", "az"), [(i * groups + j, k * groups + j) for i, j, k in pairs])
    halo_phases, halo = pl.pallas_call(
        functools.partial(halo_kernel, groups=groups, rows=rows, blocks=blocks),
        out_shape=(float_of((2, sets * half + rows, width)), float_of((2 * sets, width))),
        in_specs=[SMEM] * 2 + [VMEM],
        out_specs=(VMEM,) * 2,
        compiler_params=PARAMS,
        cost_estimate=pl.CostEstimate(flops=10**8, transcendentals=10**4, bytes_accessed=2**18),
    )(column, block, edges)
    pitch = rows + sets
    signal = pl.pallas_call(
        functools.partial(shear_kernel, groups=groups, rows=rows),
        out_shape=float_of((groups * pitch, width)),
        in_specs=[SMEM] + [VMEM] * 6,
        out_specs=VMEM,
        scratch_shapes=[pltpu.VMEM((2 * rows, width), jnp.float32)],
        compiler_params=PARAMS,
        cost_estimate=pl.CostEstimate(flops=10**9, transcendentals=0, bytes_accessed=2**21),
    )(column, signal.reshape(groups * rows, width), phases, halo, halo_phases, table, twist)
    signal = signal.reshape(groups, pitch // 2, 2, width)
    signal = lax.all_to_all(signal, "az", 0, 0, axis_index_groups=[listed(BACK, groups)], tiled=True)
    signal = signal.reshape(groups * pitch, width)
    whole_shape = (sets, row_count, width)
    remapped, radial = pl.pallas_call(
        functools.partial(derivative_kernel, groups=groups, rows=rows),
        out_shape=(float_of(whole_shape), float_of(whole_shape)),
        in_specs=[VMEM] * 2,
        out_specs=(HBM, HBM),
        scratch_shapes=[
            pltpu.VMEM(whole_shape, jnp.float32),
            pltpu.VMEM(whole_shape, jnp.float32),
            pltpu.SemaphoreType.DMA((sets + 1,)),
        ],
        compiler_params=PARAMS,
    )(signal, matrix)
    return remapped.reshape(fields.shape), radial.reshape(fields.shape)


def solution(mesh):
    return jax.shard_map(
        on_device,
        mesh=mesh,
        in_specs=(P(None, None, "rad", "az"), P("rad"), P("rad"), P("rad")),
        out_specs=(P(None, None, "rad", "az"), P(None, None, "rad", "az")),
        check_vma=False,
    )
```

```python
import functools
import math

import jax
import jax.numpy as jnp
import numpy as np
from jax import lax
from jax.experimental import pallas as pl
from jax.experimental.pallas import tpu as pltpu
from jax.sharding import PartitionSpec as P

BLOCK = 128
THERE = (43, 59)
BACK = (41, 47)
VMEM = pl.BlockSpec(memory_space=pltpu.VMEM)
SMEM = pl.BlockSpec(memory_space=pltpu.SMEM)
HBM = pl.BlockSpec(memory_space=pltpu.HBM)
PARAMS = pltpu.CompilerParams(vmem_limit_bytes=24 * 2**20)


def compact_inverse(size):
    identity = np.eye(size)
    offdiag = 0.25 * (np.eye(size, k=1) + np.eye(size, k=-1))
    inverse = identity - offdiag
    power = offdiag
    for _ in range(5):
        power = power @ power
        inverse = inverse @ (identity + power)
    return inverse.astype(np.float32)


def halves(table):
    high = np.asarray(table, np.float32).astype(jnp.bfloat16)
    low = (np.asarray(table, np.float32) - high.astype(np.float32)).astype(jnp.bfloat16)
    return high, low


def split(value):
    high = value.astype(jnp.bfloat16)
    return high, (value - high.astype(jnp.float32)).astype(jnp.bfloat16)


def dot(left, right):
    return jnp.dot(left, right, preferred_element_type=jnp.float32)


def dot3(left, right):
    return dot(left[0], right[0]) + (dot(left[0], right[1]) + dot(left[1], right[0]))


def listed(order, groups):
    first, step = order
    return [(first + step * place) % groups for place in range(groups)]


def fourier_tables(groups, width):
    half = groups // 2
    low = np.arange(half + 1)
    column = np.arange(width)
    across = 2 * np.pi * (low[:, None] * np.arange(groups)[None, :] % groups) / groups
    cosine, sine = np.cos(across), np.sin(across)
    forward = np.concatenate([cosine, -sine[1:half]])
    inverse = np.concatenate([cosine[:1], 2 * cosine[1:half], cosine[half:], -2 * sine[1:half]]).T / (groups * width)
    across = []
    for table in (forward[:, listed(THERE, groups)], inverse[listed(BACK, groups)]):
        high, low = halves(table)
        across.append(np.pad(np.concatenate([high, high, low], axis=1), ((0, 0), (0, 2 * width - 3 * groups))))
    grid = 2 * np.pi * (column[:, None] * column[None, :] % width) / width
    cosine, sine = np.cos(grid), np.sin(grid)
    along = halves(np.block([[cosine, -sine], [sine, cosine]]))
    return np.concatenate([*across, *along])


def phase_angle(signed, whole, frac, total):
    turns = ((signed * whole) & (total - 1)).astype(jnp.float32) + signed.astype(jnp.float32) * frac
    return (2.0 * math.pi / total) * turns


def prepare_kernel(
    part_ref, whole_ref, frac_ref, spacing_ref, compact_ref, table_ref,
    table_out, twist_out, phase_out, matrix_out,
    *, groups, rows,
):
    table_out[...] = table_ref[...]
    scale = 0.75 * spacing_ref[...]
    for start in range(0, scale.shape[1], BLOCK):
        here = slice(start, start + BLOCK)
        matrix_out[:BLOCK, here], matrix_out[BLOCK:, here] = split(compact_ref[...] * scale[:, here])
    half = groups // 2
    width = twist_out.shape[2]
    total = groups * width
    row_count = whole_ref.shape[1]
    shape = (half, width)
    low = lax.broadcasted_iota(jnp.int32, shape, 0)
    column = lax.broadcasted_iota(jnp.int32, shape, 1)
    angle = (2.0 * math.pi / total) * (low * column).astype(jnp.float32)
    twist_out[0, :half, :] = jnp.cos(angle)
    twist_out[1, :half, :] = jnp.sin(angle)
    edge = lax.broadcasted_iota(jnp.int32, (rows, width), 1)
    angle = (2.0 * math.pi / total) * (half * edge).astype(jnp.float32)
    twist_out[0, half:, :] = jnp.cos(angle)
    twist_out[1, half:, :] = jnp.sin(angle)
    signed = low + groups * jnp.where(column < width // 2, column, column - width)
    edge = half + groups * jnp.where(edge < width // 2, edge, edge - width)
    edge_row = lax.broadcasted_iota(jnp.int32, (rows, width), 0)
    lane = lax.broadcasted_iota(jnp.int32, (rows, row_count), 1)
    first = lax.rem(part_ref[0] * rows, row_count)
    own = lane == first + lax.broadcasted_iota(jnp.int32, (rows, row_count), 0)
    wholes = jnp.sum(jnp.where(own, whole_ref[...].astype(jnp.float32), 0.0), axis=1, keepdims=True).astype(jnp.int32)
    fracs = jnp.sum(jnp.where(own, frac_ref[...], 0.0), axis=1, keepdims=True)
    edge_angle = jnp.zeros((rows, width), jnp.float32)
    for row in range(rows):
        whole, frac = wholes[row : row + 1], fracs[row : row + 1]
        angle = phase_angle(signed, whole, frac, total)
        here = pl.ds(row * half, half)
        phase_out[0, here, :] = jnp.cos(angle)
        phase_out[1, here, :] = jnp.sin(angle)
        edge_angle = jnp.where(edge_row == row, phase_angle(edge, whole, frac, total), edge_angle)
    here = pl.ds(rows * half, rows)
    phase_out[0, here, :] = jnp.cos(edge_angle)
    phase_out[1, here, :] = jnp.sin(edge_angle)


def sheared(signals, table_ref, twist_ref, shift_cos, shift_sin, edge_ref):
    groups, width = signals[0].shape
    half = groups // 2
    edges = edge_ref.shape[0]
    size = half * len(signals)
    across, back = table_ref[:groups, : 3 * groups], table_ref[groups : 2 * groups, : 3 * groups]
    start = 2 * groups
    along_high = table_ref[start : start + 2 * width, :]
    along = jnp.concatenate([along_high, along_high, table_ref[start + 2 * width :, :]], axis=0)
    twist_cos, twist_sin = twist_ref[0, :half, :], twist_ref[1, :half, :]
    edge_cos, edge_sin = twist_ref[0, half : half + 1, :], twist_ref[1, half : half + 1, :]
    first = lax.broadcasted_iota(jnp.int32, (half, width), 0) == 0

    def stacked(blocks):
        high, low = split(jnp.concatenate(blocks, axis=1))
        return jnp.concatenate([high, low, high], axis=0)

    def transformed(value):
        high, low = split(value)
        return dot(jnp.concatenate([high, low, high], axis=1), along)

    signal = dot(across, stacked(signals))
    blocks = []
    edge_ref[...] = jnp.zeros_like(edge_ref)
    for row in range(len(signals)):
        here = slice(row * width, (row + 1) * width)
        real, imag = signal[:half, here], signal[half:, here]
        edge_ref[pl.ds(row, 1), :] = imag[:1, :]
        imag = jnp.where(first, 0.0, imag)
        blocks.append(
            jnp.concatenate([real * twist_cos + imag * twist_sin, imag * twist_cos - real * twist_sin], axis=1)
        )
    edge = edge_ref[...]
    edge = jnp.concatenate([edge * edge_cos, -edge * edge_sin], axis=1)
    spectrum = transformed(jnp.concatenate([*blocks, edge], axis=0))
    real, imag = spectrum[:, :width], spectrum[:, width:]
    spectrum = jnp.concatenate([real * shift_cos + imag * shift_sin, real * shift_sin - imag * shift_cos], axis=1)
    spectrum = transformed(spectrum)
    edge = spectrum[size:, :]
    edge_ref[...] = edge[:, :width] * edge_cos + edge[:, width:] * edge_sin
    blocks = []
    for row in range(len(signals)):
        here = slice(row * half, (row + 1) * half)
        real, imag = spectrum[here, :width], spectrum[here, width:]
        edge = jnp.broadcast_to(edge_ref[pl.ds(row, 1), :], (half, width))
        parts = [real * twist_cos + imag * twist_sin, jnp.where(first, edge, real * twist_sin - imag * twist_cos)]
        blocks.append(jnp.concatenate(parts, axis=0))
    return dot(back, stacked(blocks))


def edge_kernel(position_ref, cells_ref, keep_out, give_out, tiles, sems):
    sets, row_count, width = cells_ref.shape
    depth = tiles.shape[2]
    loads = []
    for side, start in enumerate((row_count - depth, 0)):
        for field in range(sets):
            source = cells_ref.at[field, pl.ds(start, depth)]
            loads.append(pltpu.make_async_copy(source, tiles.at[side, field], sems.at[side, field]))
            loads[-1].start()
    for load in loads:
        load.wait()
    is_odd = position_ref[0] & 1 == 1
    last = [tiles[0, field, depth - 1 :, :] for field in range(sets)]
    first = [tiles[1, field, :1, :] for field in range(sets)]
    keep = [jnp.where(is_odd, theirs, ours) for ours, theirs in zip(last, first, strict=True)]
    keep_out[...] = jnp.concatenate(keep, axis=0)
    give_out[...] = jnp.concatenate([jnp.where(is_odd, ours, theirs) for ours, theirs in zip(last, first, strict=True)], axis=0)


def join_kernel(position_ref, whole_ref, frac_ref, _, keep_ref, got_ref, out_ref):
    sets, width = keep_ref.shape
    is_odd = position_ref[0] & 1 == 1
    last = whole_ref.shape[1] - 1
    out_ref[...] = jnp.zeros_like(out_ref)
    out_ref[pl.ds(0, sets), :] = keep_ref[...]
    out_ref[pl.ds(sets, sets), :] = got_ref[...]
    for place, ref in enumerate((whole_ref, frac_ref)):
        shift = jnp.where(is_odd, ref[:, :1].astype(jnp.float32), ref[:, last:].astype(jnp.float32))
        out_ref[pl.ds(2 * sets + place, 1), :] = jnp.broadcast_to(shift, (1, width))


def halo_kernel(position_ref, block_ref, edges_ref, phase_out, halo_out, *, groups, rows, blocks):
    is_odd = position_ref[0] & 1 == 1
    is_end = jnp.where(is_odd, block_ref[0] == blocks - 1, block_ref[0] == 0)
    cells = edges_ref[...]
    sets = halo_out.shape[0] // 2
    keep, got = cells[:sets], cells[sets : 2 * sets]
    both = jnp.where(is_odd, jnp.concatenate([got, keep], axis=0), jnp.concatenate([keep, got], axis=0))
    halo_out[...] = jnp.where(is_end, 0.0, both)
    whole, frac = cells[2 * sets : 2 * sets + 1].astype(jnp.int32), cells[2 * sets + 1 : 2 * sets + 2]
    width = phase_out.shape[2]
    half = groups // 2
    shape = (half, width)
    low = lax.broadcasted_iota(jnp.int32, shape, 0)
    column = lax.broadcasted_iota(jnp.int32, shape, 1)
    signed = low + groups * jnp.where(column < width // 2, column, column - width)
    edge = lax.broadcasted_iota(jnp.int32, (rows, width), 1)
    edge = half + groups * jnp.where(edge < width // 2, edge, edge - width)
    angle, edge_angle = [phase_angle(place, whole, frac, groups * width) for place in (signed, edge)]
    for part, wave in enumerate((jnp.cos, jnp.sin)):
        shift = wave(angle)
        for field in range(sets):
            phase_out[part, pl.ds(field * half, half), :] = shift
        phase_out[part, pl.ds(sets * half, rows), :] = wave(edge_angle)


def shear_kernel(
    position_ref, signal_ref, phase_ref, halo_ref, halo_phase_ref, table_ref, twist_ref, out_ref, edge_ref,
    *, groups, rows,
):
    sets = halo_ref.shape[0] // 2
    pitch = rows + sets
    half = groups // 2
    signals = [signal_ref[pl.ds(row, groups, stride=rows), :] for row in range(rows)]
    width = signals[0].shape[1]
    first, step = THERE
    group = (first + step * lax.broadcasted_iota(jnp.int32, (groups, width), 0)) & (groups - 1)
    group -= position_ref[0] & -2
    for field in range(sets):
        even, odd = halo_ref[field : field + 1, :], halo_ref[sets + field : sets + field + 1, :]
        signals.append(jnp.where(group == 0, even, jnp.where(group == 1, odd, 0.0)))
    shifts = []
    for part in range(2):
        ours, theirs = phase_ref[part], halo_phase_ref[part]
        cut, halo_cut = rows * half, sets * half
        shifts.append(jnp.concatenate([ours[:cut], theirs[:halo_cut], ours[cut:], theirs[halo_cut:]], axis=0))
    signal = sheared(signals, table_ref, twist_ref, *shifts, edge_ref)
    for row in range(pitch):
        out_ref[pl.ds(row, groups, stride=pitch), :] = signal[:, row * width : (row + 1) * width]


def derivative_kernel(
    cells_ref, matrix_ref, remapped_out, radial_out, remapped, radial, sems, *, groups, rows
):
    field_count, row_count, width = remapped.shape
    pitch = cells_ref.shape[0] // groups
    parts = row_count // rows
    there, back = listed(THERE, groups), listed(BACK, groups)
    for place, group in enumerate(back):
        part = there.index(group)
        here = pl.ds(part % parts * rows, rows)
        remapped[part // parts, here, :] = cells_ref[pl.ds(place * pitch, rows), :]
    stores = [pltpu.make_async_copy(remapped, remapped_out, sems.at[field_count])]
    stores[0].start()

    def total(place):
        return jnp.sum(cells_ref[pl.ds(place, groups // 2, stride=2 * pitch), :], axis=0, keepdims=True)

    before = [total(back[0] % 2 * pitch + rows + field) for field in range(field_count)]
    after = [total((1 - back[0] % 2) * pitch + rows + field) for field in range(field_count)]

    row = lax.broadcasted_iota(jnp.int32, (row_count, width), 0)
    for field in range(field_count):
        cells = remapped[field]
        above = jnp.where(row == 0, 0.0, pltpu.roll(cells, 1, 0))
        below = jnp.where(row == row_count - 1, 0.0, pltpu.roll(cells, row_count - 1, 0))
        high, low = split(below - above)
        for start in range(0, row_count, BLOCK):
            here = slice(start, start + BLOCK)
            matrix = (matrix_ref[:BLOCK, here], matrix_ref[BLOCK:, here])
            result = dot3(matrix, (high[here], low[here]))
            if start == 0:
                result -= (matrix[0][:, :1].astype(jnp.float32) + matrix[1][:, :1].astype(jnp.float32)) * before[field]
            if start == row_count - BLOCK:
                result += (matrix[0][:, -1:].astype(jnp.float32) + matrix[1][:, -1:].astype(jnp.float32)) * after[field]
            radial[field, here, :] = result
        stores.append(pltpu.make_async_copy(radial.at[field], radial_out.at[field], sems.at[field]))
        stores[-1].start()
    for store in stores:
        store.wait()


def on_device(fields, whole_shift, frac_shift, inv_spacing):
    groups = lax.axis_size("az")
    blocks = lax.axis_size("rad")
    column = lax.axis_index("az").astype(jnp.int32).reshape(1)
    part = (column - THERE[0]) * pow(THERE[1], -1, groups) & (groups - 1)
    block = lax.axis_index("rad").astype(jnp.int32).reshape(1)
    field_count, plane_count, row_count, width = fields.shape
    sets = field_count * plane_count
    rows = sets * row_count // groups
    half = groups // 2
    table = fourier_tables(groups, width)
    shifts = [row.reshape(1, row_count) for row in (whole_shift, frac_shift, inv_spacing)]
    float_of = functools.partial(jax.ShapeDtypeStruct, dtype=jnp.float32)

    signal = lax.all_to_all(
        fields.reshape(groups, rows, width), "az", 0, 0, axis_index_groups=[listed(THERE, groups)], tiled=True
    )
    table, twist, phases, matrix = pl.pallas_call(
        functools.partial(prepare_kernel, groups=groups, rows=rows),
        out_shape=(
            jax.ShapeDtypeStruct(table.shape, jnp.bfloat16),
            float_of((2, half + rows, width)),
            float_of((2, (half + 1) * rows, width)),
            jax.ShapeDtypeStruct((2 * BLOCK, row_count), jnp.bfloat16),
        ),
        in_specs=[SMEM] + [VMEM] * 5,
        out_specs=(VMEM,) * 4,
        compiler_params=PARAMS,
        cost_estimate=pl.CostEstimate(flops=10**9, transcendentals=10**5, bytes_accessed=2**21),
    )(
        part,
        *shifts,
        jnp.asarray(compact_inverse(BLOCK)),
        jnp.asarray(table),
    )
    planes = fields.reshape(sets, row_count, width)
    keep, give = pl.pallas_call(
        edge_kernel,
        out_shape=(float_of((sets, width)),) * 2,
        in_specs=[SMEM, HBM],
        out_specs=(VMEM,) * 2,
        scratch_shapes=[pltpu.VMEM((2, sets, 8, width), jnp.float32), pltpu.SemaphoreType.DMA((2, sets))],
        compiler_params=PARAMS,
    )(column, planes)
    got = lax.ppermute(give, "az", [(i, i ^ 1) for i in range(groups)])
    edges = pl.pallas_call(
        join_kernel,
        out_shape=float_of((8, width)),
        in_specs=[SMEM] + [VMEM] * 5,
        out_specs=VMEM,
        compiler_params=PARAMS,
    )(column, *shifts, keep, got)
    turns = []
    for place in range(blocks * groups):
        step = -groups if place % 2 else groups
        turns.append((place, place + step if 0 <= place + step < blocks * groups else place ^ 1))
    edges = lax.ppermute(edges, ("rad", "az"), turns)
    halo_phases, halo = pl.pallas_call(
        functools.partial(halo_kernel, groups=groups, rows=rows, blocks=blocks),
        out_shape=(float_of((2, sets * half + rows, width)), float_of((2 * sets, width))),
        in_specs=[SMEM] * 2 + [VMEM],
        out_specs=(VMEM,) * 2,
        compiler_params=PARAMS,
        cost_estimate=pl.CostEstimate(flops=10**8, transcendentals=10**4, bytes_accessed=2**18),
    )(column, block, edges)
    pitch = rows + sets
    signal = pl.pallas_call(
        functools.partial(shear_kernel, groups=groups, rows=rows),
        out_shape=float_of((groups * pitch, width)),
        in_specs=[SMEM] + [VMEM] * 6,
        out_specs=VMEM,
        scratch_shapes=[pltpu.VMEM((2 * rows, width), jnp.float32)],
        compiler_params=PARAMS,
        cost_estimate=pl.CostEstimate(flops=10**9, transcendentals=0, bytes_accessed=2**21),
    )(column, signal.reshape(groups * rows, width), phases, halo, halo_phases, table, twist)
    signal = signal.reshape(groups, pitch // 2, 2, width)
    signal = lax.all_to_all(signal, "az", 0, 0, axis_index_groups=[listed(BACK, groups)], tiled=True)
    signal = signal.reshape(groups * pitch, width)
    whole_shape = (sets, row_count, width)
    remapped, radial = pl.pallas_call(
        functools.partial(derivative_kernel, groups=groups, rows=rows),
        out_shape=(float_of(whole_shape), float_of(whole_shape)),
        in_specs=[VMEM] * 2,
        out_specs=(HBM, HBM),
        scratch_shapes=[
            pltpu.VMEM(whole_shape, jnp.float32),
            pltpu.VMEM(whole_shape, jnp.float32),
            pltpu.SemaphoreType.DMA((sets + 1,)),
        ],
        compiler_params=PARAMS,
    )(signal, matrix)
    return remapped.reshape(fields.shape), radial.reshape(fields.shape)


def solution(mesh):
    return jax.shard_map(
        on_device,
        mesh=mesh,
        in_specs=(P(None, None, "rad", "az"), P("rad"), P("rad"), P("rad")),
        out_specs=(P(None, None, "rad", "az"), P(None, None, "rad", "az")),
        check_vma=False,
    )
```

```python
import functools
import math

import jax
import jax.numpy as jnp
import numpy as np
from jax import lax
from jax.experimental import pallas as pl
from jax.experimental.pallas import tpu as pltpu
from jax.sharding import PartitionSpec as P

BLOCK = 128
THERE = (43, 5)
BACK = (43, 59)
VMEM = pl.BlockSpec(memory_space=pltpu.VMEM)
SMEM = pl.BlockSpec(memory_space=pltpu.SMEM)
HBM = pl.BlockSpec(memory_space=pltpu.HBM)
PARAMS = pltpu.CompilerParams(vmem_limit_bytes=24 * 2**20)


def compact_inverse(size):
    identity = np.eye(size)
    offdiag = 0.25 * (np.eye(size, k=1) + np.eye(size, k=-1))
    inverse = identity - offdiag
    power = offdiag
    for _ in range(5):
        power = power @ power
        inverse = inverse @ (identity + power)
    return inverse.astype(np.float32)


def halves(table):
    high = np.asarray(table, np.float32).astype(jnp.bfloat16)
    low = (np.asarray(table, np.float32) - high.astype(np.float32)).astype(jnp.bfloat16)
    return high, low


def split(value):
    high = value.astype(jnp.bfloat16)
    return high, (value - high.astype(jnp.float32)).astype(jnp.bfloat16)


def dot(left, right):
    return jnp.dot(left, right, preferred_element_type=jnp.float32)


def dot3(left, right):
    return dot(left[0], right[0]) + (dot(left[0], right[1]) + dot(left[1], right[0]))


def listed(order, groups):
    first, step = order
    return [(first + step * place) % groups for place in range(groups)]


def fourier_tables(groups, width):
    half = groups // 2
    low = np.arange(half + 1)
    column = np.arange(width)
    across = 2 * np.pi * (low[:, None] * np.arange(groups)[None, :] % groups) / groups
    cosine, sine = np.cos(across), np.sin(across)
    forward = np.concatenate([cosine, -sine[1:half]])
    inverse = np.concatenate([cosine[:1], 2 * cosine[1:half], cosine[half:], -2 * sine[1:half]]).T / (groups * width)
    across = []
    for table in (forward[:, listed(THERE, groups)], inverse[listed(BACK, groups)]):
        high, low = halves(table)
        across.append(np.pad(np.concatenate([high, high, low], axis=1), ((0, 0), (0, 2 * width - 3 * groups))))
    grid = 2 * np.pi * (column[:, None] * column[None, :] % width) / width
    cosine, sine = np.cos(grid), np.sin(grid)
    along = halves(np.block([[cosine, -sine], [sine, cosine]]))
    return np.concatenate([*across, *along])


def phase_angle(signed, whole, frac, total):
    turns = ((signed * whole) & (total - 1)).astype(jnp.float32) + signed.astype(jnp.float32) * frac
    return (2.0 * math.pi / total) * turns


def prepare_kernel(
    part_ref, whole_ref, frac_ref, spacing_ref, compact_ref, table_ref,
    table_out, twist_out, phase_out, matrix_out,
    *, groups, rows,
):
    table_out[...] = table_ref[...]
    scale = 0.75 * spacing_ref[...]
    for start in range(0, scale.shape[1], BLOCK):
        here = slice(start, start + BLOCK)
        matrix_out[:BLOCK, here], matrix_out[BLOCK:, here] = split(compact_ref[...] * scale[:, here])
    half = groups // 2
    width = twist_out.shape[2]
    total = groups * width
    row_count = whole_ref.shape[1]
    shape = (half, width)
    low = lax.broadcasted_iota(jnp.int32, shape, 0)
    column = lax.broadcasted_iota(jnp.int32, shape, 1)
    angle = (2.0 * math.pi / total) * (low * column).astype(jnp.float32)
    twist_out[0, :half, :] = jnp.cos(angle)
    twist_out[1, :half, :] = jnp.sin(angle)
    edge = lax.broadcasted_iota(jnp.int32, (rows, width), 1)
    angle = (2.0 * math.pi / total) * (half * edge).astype(jnp.float32)
    twist_out[0, half:, :] = jnp.cos(angle)
    twist_out[1, half:, :] = jnp.sin(angle)
    signed = low + groups * jnp.where(column < width // 2, column, column - width)
    edge = half + groups * jnp.where(edge < width // 2, edge, edge - width)
    edge_row = lax.broadcasted_iota(jnp.int32, (rows, width), 0)
    lane = lax.broadcasted_iota(jnp.int32, (rows, row_count), 1)
    first = lax.rem(part_ref[0] * rows, row_count)
    own = lane == first + lax.broadcasted_iota(jnp.int32, (rows, row_count), 0)
    wholes = jnp.sum(jnp.where(own, whole_ref[...].astype(jnp.float32), 0.0), axis=1, keepdims=True).astype(jnp.int32)
    fracs = jnp.sum(jnp.where(own, frac_ref[...], 0.0), axis=1, keepdims=True)
    edge_angle = jnp.zeros((rows, width), jnp.float32)
    for row in range(rows):
        whole, frac = wholes[row : row + 1], fracs[row : row + 1]
        angle = phase_angle(signed, whole, frac, total)
        here = pl.ds(row * half, half)
        phase_out[0, here, :] = jnp.cos(angle)
        phase_out[1, here, :] = jnp.sin(angle)
        edge_angle = jnp.where(edge_row == row, phase_angle(edge, whole, frac, total), edge_angle)
    here = pl.ds(rows * half, rows)
    phase_out[0, here, :] = jnp.cos(edge_angle)
    phase_out[1, here, :] = jnp.sin(edge_angle)


def sheared(signals, table_ref, twist_ref, shift_cos, shift_sin, edge_ref):
    groups, width = signals[0].shape
    half = groups // 2
    edges = edge_ref.shape[0]
    size = half * len(signals)
    across, back = table_ref[:groups, : 3 * groups], table_ref[groups : 2 * groups, : 3 * groups]
    start = 2 * groups
    along_high = table_ref[start : start + 2 * width, :]
    along = jnp.concatenate([along_high, along_high, table_ref[start + 2 * width :, :]], axis=0)
    twist_cos, twist_sin = twist_ref[0, :half, :], twist_ref[1, :half, :]
    edge_cos, edge_sin = twist_ref[0, half : half + 1, :], twist_ref[1, half : half + 1, :]
    first = lax.broadcasted_iota(jnp.int32, (half, width), 0) == 0

    def stacked(blocks):
        high, low = split(jnp.concatenate(blocks, axis=1))
        return jnp.concatenate([high, low, high], axis=0)

    def transformed(value):
        high, low = split(value)
        return dot(jnp.concatenate([high, low, high], axis=1), along)

    signal = dot(across, stacked(signals))
    blocks = []
    edge_ref[...] = jnp.zeros_like(edge_ref)
    for row in range(len(signals)):
        here = slice(row * width, (row + 1) * width)
        real, imag = signal[:half, here], signal[half:, here]
        edge_ref[pl.ds(row, 1), :] = imag[:1, :]
        imag = jnp.where(first, 0.0, imag)
        blocks.append(
            jnp.concatenate([real * twist_cos + imag * twist_sin, imag * twist_cos - real * twist_sin], axis=1)
        )
    edge = edge_ref[...]
    edge = jnp.concatenate([edge * edge_cos, -edge * edge_sin], axis=1)
    spectrum = transformed(jnp.concatenate([*blocks, edge], axis=0))
    real, imag = spectrum[:, :width], spectrum[:, width:]
    spectrum = jnp.concatenate([real * shift_cos + imag * shift_sin, real * shift_sin - imag * shift_cos], axis=1)
    spectrum = transformed(spectrum)
    edge = spectrum[size:, :]
    edge_ref[...] = edge[:, :width] * edge_cos + edge[:, width:] * edge_sin
    blocks = []
    for row in range(len(signals)):
        here = slice(row * half, (row + 1) * half)
        real, imag = spectrum[here, :width], spectrum[here, width:]
        edge = jnp.broadcast_to(edge_ref[pl.ds(row, 1), :], (half, width))
        parts = [real * twist_cos + imag * twist_sin, jnp.where(first, edge, real * twist_sin - imag * twist_cos)]
        blocks.append(jnp.concatenate(parts, axis=0))
    return dot(back, stacked(blocks))


def edge_kernel(position_ref, cells_ref, keep_out, give_out, tiles, sems):
    sets, row_count, width = cells_ref.shape
    depth = tiles.shape[2]
    loads = []
    for side, start in enumerate((row_count - depth, 0)):
        for field in range(sets):
            source = cells_ref.at[field, pl.ds(start, depth)]
            loads.append(pltpu.make_async_copy(source, tiles.at[side, field], sems.at[side, field]))
            loads[-1].start()
    for load in loads:
        load.wait()
    is_odd = position_ref[0] & 1 == 1
    last = [tiles[0, field, depth - 1 :, :] for field in range(sets)]
    first = [tiles[1, field, :1, :] for field in range(sets)]
    keep = [jnp.where(is_odd, theirs, ours) for ours, theirs in zip(last, first, strict=True)]
    keep_out[...] = jnp.concatenate(keep, axis=0)
    give_out[...] = jnp.concatenate([jnp.where(is_odd, ours, theirs) for ours, theirs in zip(last, first, strict=True)], axis=0)


def join_kernel(position_ref, whole_ref, frac_ref, _, keep_ref, got_ref, out_ref):
    sets, width = keep_ref.shape
    is_odd = position_ref[0] & 1 == 1
    last = whole_ref.shape[1] - 1
    out_ref[...] = jnp.zeros_like(out_ref)
    out_ref[pl.ds(0, sets), :] = keep_ref[...]
    out_ref[pl.ds(sets, sets), :] = got_ref[...]
    for place, ref in enumerate((whole_ref, frac_ref)):
        shift = jnp.where(is_odd, ref[:, :1].astype(jnp.float32), ref[:, last:].astype(jnp.float32))
        out_ref[pl.ds(2 * sets + place, 1), :] = jnp.broadcast_to(shift, (1, width))


def halo_kernel(position_ref, block_ref, edges_ref, phase_out, halo_out, *, groups, rows, blocks):
    is_odd = position_ref[0] & 1 == 1
    is_end = jnp.where(is_odd, block_ref[0] == blocks - 1, block_ref[0] == 0)
    cells = edges_ref[...]
    sets = halo_out.shape[0] // 2
    keep, got = cells[:sets], cells[sets : 2 * sets]
    both = jnp.where(is_odd, jnp.concatenate([got, keep], axis=0), jnp.concatenate([keep, got], axis=0))
    halo_out[...] = jnp.where(is_end, 0.0, both)
    whole, frac = cells[2 * sets : 2 * sets + 1].astype(jnp.int32), cells[2 * sets + 1 : 2 * sets + 2]
    width = phase_out.shape[2]
    half = groups // 2
    shape = (half, width)
    low = lax.broadcasted_iota(jnp.int32, shape, 0)
    column = lax.broadcasted_iota(jnp.int32, shape, 1)
    signed = low + groups * jnp.where(column < width // 2, column, column - width)
    edge = lax.broadcasted_iota(jnp.int32, (rows, width), 1)
    edge = half + groups * jnp.where(edge < width // 2, edge, edge - width)
    angle, edge_angle = [phase_angle(place, whole, frac, groups * width) for place in (signed, edge)]
    for part, wave in enumerate((jnp.cos, jnp.sin)):
        shift = wave(angle)
        for field in range(sets):
            phase_out[part, pl.ds(field * half, half), :] = shift
        phase_out[part, pl.ds(sets * half, rows), :] = wave(edge_angle)


def shear_kernel(
    position_ref, signal_ref, phase_ref, halo_ref, halo_phase_ref, table_ref, twist_ref, out_ref, edge_ref,
    *, groups, rows,
):
    sets = halo_ref.shape[0] // 2
    pitch = rows + sets
    half = groups // 2
    signals = [signal_ref[pl.ds(row, groups, stride=rows), :] for row in range(rows)]
    width = signals[0].shape[1]
    first, step = THERE
    group = (first + step * lax.broadcasted_iota(jnp.int32, (groups, width), 0)) & (groups - 1)
    group -= position_ref[0] & -2
    for field in range(sets):
        even, odd = halo_ref[field : field + 1, :], halo_ref[sets + field : sets + field + 1, :]
        signals.append(jnp.where(group == 0, even, jnp.where(group == 1, odd, 0.0)))
    shifts = []
    for part in range(2):
        ours, theirs = phase_ref[part], halo_phase_ref[part]
        cut, halo_cut = rows * half, sets * half
        shifts.append(jnp.concatenate([ours[:cut], theirs[:halo_cut], ours[cut:], theirs[halo_cut:]], axis=0))
    signal = sheared(signals, table_ref, twist_ref, *shifts, edge_ref)
    for row in range(pitch):
        out_ref[pl.ds(row, groups, stride=pitch), :] = signal[:, row * width : (row + 1) * width]


def derivative_kernel(
    cells_ref, matrix_ref, remapped_out, radial_out, remapped, radial, sems, *, groups, rows
):
    field_count, row_count, width = remapped.shape
    pitch = cells_ref.shape[0] // groups
    parts = row_count // rows
    there, back = listed(THERE, groups), listed(BACK, groups)
    for place, group in enumerate(back):
        part = there.index(group)
        here = pl.ds(part % parts * rows, rows)
        remapped[part // parts, here, :] = cells_ref[pl.ds(place * pitch, rows), :]
    stores = [pltpu.make_async_copy(remapped, remapped_out, sems.at[field_count])]
    stores[0].start()

    def total(place):
        return jnp.sum(cells_ref[pl.ds(place, groups // 2, stride=2 * pitch), :], axis=0, keepdims=True)

    before = [total(back[0] % 2 * pitch + rows + field) for field in range(field_count)]
    after = [total((1 - back[0] % 2) * pitch + rows + field) for field in range(field_count)]

    row = lax.broadcasted_iota(jnp.int32, (row_count, width), 0)
    for field in range(field_count):
        cells = remapped[field]
        above = jnp.where(row == 0, 0.0, pltpu.roll(cells, 1, 0))
        below = jnp.where(row == row_count - 1, 0.0, pltpu.roll(cells, row_count - 1, 0))
        high, low = split(below - above)
        for start in range(0, row_count, BLOCK):
            here = slice(start, start + BLOCK)
            matrix = (matrix_ref[:BLOCK, here], matrix_ref[BLOCK:, here])
            result = dot3(matrix, (high[here], low[here]))
            if start == 0:
                result -= (matrix[0][:, :1].astype(jnp.float32) + matrix[1][:, :1].astype(jnp.float32)) * before[field]
            if start == row_count - BLOCK:
                result += (matrix[0][:, -1:].astype(jnp.float32) + matrix[1][:, -1:].astype(jnp.float32)) * after[field]
            radial[field, here, :] = result
        stores.append(pltpu.make_async_copy(radial.at[field], radial_out.at[field], sems.at[field]))
        stores[-1].start()
    for store in stores:
        store.wait()


def on_device(fields, whole_shift, frac_shift, inv_spacing):
    groups = lax.axis_size("az")
    blocks = lax.axis_size("rad")
    column = lax.axis_index("az").astype(jnp.int32).reshape(1)
    part = (column - THERE[0]) * pow(THERE[1], -1, groups) & (groups - 1)
    block = lax.axis_index("rad").astype(jnp.int32).reshape(1)
    field_count, plane_count, row_count, width = fields.shape
    sets = field_count * plane_count
    rows = sets * row_count // groups
    half = groups // 2
    table = fourier_tables(groups, width)
    shifts = [row.reshape(1, row_count) for row in (whole_shift, frac_shift, inv_spacing)]
    float_of = functools.partial(jax.ShapeDtypeStruct, dtype=jnp.float32)

    signal = lax.all_to_all(
        fields.reshape(groups, rows, width), "az", 0, 0, axis_index_groups=[listed(THERE, groups)], tiled=True
    )
    table, twist, phases, matrix = pl.pallas_call(
        functools.partial(prepare_kernel, groups=groups, rows=rows),
        out_shape=(
            jax.ShapeDtypeStruct(table.shape, jnp.bfloat16),
            float_of((2, half + rows, width)),
            float_of((2, (half + 1) * rows, width)),
            jax.ShapeDtypeStruct((2 * BLOCK, row_count), jnp.bfloat16),
        ),
        in_specs=[SMEM] + [VMEM] * 5,
        out_specs=(VMEM,) * 4,
        compiler_params=PARAMS,
        cost_estimate=pl.CostEstimate(flops=10**9, transcendentals=10**5, bytes_accessed=2**21),
    )(
        part,
        *shifts,
        jnp.asarray(compact_inverse(BLOCK)),
        jnp.asarray(table),
    )
    planes = fields.reshape(sets, row_count, width)
    keep, give = pl.pallas_call(
        edge_kernel,
        out_shape=(float_of((sets, width)),) * 2,
        in_specs=[SMEM, HBM],
        out_specs=(VMEM,) * 2,
        scratch_shapes=[pltpu.VMEM((2, sets, 8, width), jnp.float32), pltpu.SemaphoreType.DMA((2, sets))],
        compiler_params=PARAMS,
    )(column, planes)
    got = lax.ppermute(give, "az", [(i, i ^ 1) for i in range(groups)])
    edges = pl.pallas_call(
        join_kernel,
        out_shape=float_of((8, width)),
        in_specs=[SMEM] + [VMEM] * 5,
        out_specs=VMEM,
        compiler_params=PARAMS,
    )(column, *shifts, keep, got)
    turns = []
    for place in range(blocks * groups):
        step = -groups if place % 2 else groups
        turns.append((place, place + step if 0 <= place + step < blocks * groups else place ^ 1))
    edges = lax.ppermute(edges, ("rad", "az"), turns)
    halo_phases, halo = pl.pallas_call(
        functools.partial(halo_kernel, groups=groups, rows=rows, blocks=blocks),
        out_shape=(float_of((2, sets * half + rows, width)), float_of((2 * sets, width))),
        in_specs=[SMEM] * 2 + [VMEM],
        out_specs=(VMEM,) * 2,
        compiler_params=PARAMS,
        cost_estimate=pl.CostEstimate(flops=10**8, transcendentals=10**4, bytes_accessed=2**18),
    )(column, block, edges)
    pitch = rows + sets
    signal = pl.pallas_call(
        functools.partial(shear_kernel, groups=groups, rows=rows),
        out_shape=float_of((groups * pitch, width)),
        in_specs=[SMEM] + [VMEM] * 6,
        out_specs=VMEM,
        scratch_shapes=[pltpu.VMEM((2 * rows, width), jnp.float32)],
        compiler_params=PARAMS,
        cost_estimate=pl.CostEstimate(flops=10**9, transcendentals=0, bytes_accessed=2**21),
    )(column, signal.reshape(groups * rows, width), phases, halo, halo_phases, table, twist)
    signal = signal.reshape(groups, pitch // 2, 2, width)
    signal = lax.all_to_all(signal, "az", 0, 0, axis_index_groups=[listed(BACK, groups)], tiled=True)
    signal = signal.reshape(groups * pitch, width)
    whole_shape = (sets, row_count, width)
    remapped, radial = pl.pallas_call(
        functools.partial(derivative_kernel, groups=groups, rows=rows),
        out_shape=(float_of(whole_shape), float_of(whole_shape)),
        in_specs=[VMEM] * 2,
        out_specs=(HBM, HBM),
        scratch_shapes=[
            pltpu.VMEM(whole_shape, jnp.float32),
            pltpu.VMEM(whole_shape, jnp.float32),
            pltpu.SemaphoreType.DMA((sets + 1,)),
        ],
        compiler_params=PARAMS,
    )(signal, matrix)
    return remapped.reshape(fields.shape), radial.reshape(fields.shape)


def solution(mesh):
    return jax.shard_map(
        on_device,
        mesh=mesh,
        in_specs=(P(None, None, "rad", "az"), P("rad"), P("rad"), P("rad")),
        out_specs=(P(None, None, "rad", "az"), P(None, None, "rad", "az")),
        check_vma=False,
    )
```

```python
import functools
import math

import jax
import jax.numpy as jnp
import numpy as np
from jax import lax
from jax.experimental import pallas as pl
from jax.experimental.pallas import tpu as pltpu
from jax.sharding import PartitionSpec as P

BLOCK = 128
QUAD = 4
THERE = (43, 5)
BACK = (43, 59)
VMEM = pl.BlockSpec(memory_space=pltpu.VMEM)
SMEM = pl.BlockSpec(memory_space=pltpu.SMEM)
HBM = pl.BlockSpec(memory_space=pltpu.HBM)
PARAMS = pltpu.CompilerParams(vmem_limit_bytes=24 * 2**20)


def compact_inverse(size):
    identity = np.eye(size)
    offdiag = 0.25 * (np.eye(size, k=1) + np.eye(size, k=-1))
    inverse = identity - offdiag
    power = offdiag
    for _ in range(5):
        power = power @ power
        inverse = inverse @ (identity + power)
    return inverse.astype(np.float32)


def halves(table):
    high = np.asarray(table, np.float32).astype(jnp.bfloat16)
    low = (np.asarray(table, np.float32) - high.astype(np.float32)).astype(jnp.bfloat16)
    return high, low


def split(value):
    high = value.astype(jnp.bfloat16)
    return high, (value - high.astype(jnp.float32)).astype(jnp.bfloat16)


def dot(left, right):
    return jnp.dot(left, right, preferred_element_type=jnp.float32)


def dot3(left, right):
    return dot(left[0], right[0]) + (dot(left[0], right[1]) + dot(left[1], right[0]))


def listed(order, groups):
    first, step = order
    return [(first + step * place) % groups for place in range(groups)]


def fourier_tables(groups, width):
    half = groups // 2
    low = np.arange(half + 1)
    column = np.arange(width)
    across = 2 * np.pi * (low[:, None] * np.arange(groups)[None, :] % groups) / groups
    cosine, sine = np.cos(across), np.sin(across)
    forward = np.concatenate([cosine, -sine[1:half]])
    inverse = np.concatenate([cosine[:1], 2 * cosine[1:half], cosine[half:], -2 * sine[1:half]]).T / (groups * width)
    across = []
    for table in (forward[:, listed(THERE, groups)], inverse[listed(BACK, groups)]):
        high, low = halves(table)
        across.append(np.pad(np.concatenate([high, high, low], axis=1), ((0, 0), (0, 2 * width - 3 * groups))))
    grid = 2 * np.pi * (column[:, None] * column[None, :] % width) / width
    cosine, sine = np.cos(grid), np.sin(grid)
    along = halves(np.block([[cosine, -sine], [sine, cosine]]))
    return np.concatenate([*across, *along])


def phase_angle(signed, whole, frac, total):
    turns = ((signed * whole) & (total - 1)).astype(jnp.float32) + signed.astype(jnp.float32) * frac
    return (2.0 * math.pi / total) * turns


def prepare_kernel(
    part_ref, whole_ref, frac_ref, spacing_ref, compact_ref, table_ref,
    table_out, twist_out, phase_out, matrix_out,
    *, groups, rows,
):
    table_out[...] = table_ref[...]
    scale = 0.75 * spacing_ref[...]
    for start in range(0, scale.shape[1], BLOCK):
        here = slice(start, start + BLOCK)
        matrix_out[:BLOCK, here], matrix_out[BLOCK:, here] = split(compact_ref[...] * scale[:, here])
    half = groups // 2
    width = twist_out.shape[2]
    total = groups * width
    row_count = whole_ref.shape[1]
    shape = (half, width)
    low = lax.broadcasted_iota(jnp.int32, shape, 0)
    column = lax.broadcasted_iota(jnp.int32, shape, 1)
    angle = (2.0 * math.pi / total) * (low * column).astype(jnp.float32)
    twist_out[0, :half, :] = jnp.cos(angle)
    twist_out[1, :half, :] = jnp.sin(angle)
    edge = lax.broadcasted_iota(jnp.int32, (rows, width), 1)
    angle = (2.0 * math.pi / total) * (half * edge).astype(jnp.float32)
    twist_out[0, half:, :] = jnp.cos(angle)
    twist_out[1, half:, :] = jnp.sin(angle)
    signed = low + groups * jnp.where(column < width // 2, column, column - width)
    edge = half + groups * jnp.where(edge < width // 2, edge, edge - width)
    edge_row = lax.broadcasted_iota(jnp.int32, (rows, width), 0)
    lane = lax.broadcasted_iota(jnp.int32, (rows, row_count), 1)
    first = lax.rem(part_ref[0] * rows, row_count)
    own = lane == first + lax.broadcasted_iota(jnp.int32, (rows, row_count), 0)
    wholes = jnp.sum(jnp.where(own, whole_ref[...].astype(jnp.float32), 0.0), axis=1, keepdims=True).astype(jnp.int32)
    fracs = jnp.sum(jnp.where(own, frac_ref[...], 0.0), axis=1, keepdims=True)
    edge_angle = jnp.zeros((rows, width), jnp.float32)
    for row in range(rows):
        whole, frac = wholes[row : row + 1], fracs[row : row + 1]
        angle = phase_angle(signed, whole, frac, total)
        here = pl.ds(row * half, half)
        phase_out[0, here, :] = jnp.cos(angle)
        phase_out[1, here, :] = jnp.sin(angle)
        edge_angle = jnp.where(edge_row == row, phase_angle(edge, whole, frac, total), edge_angle)
    here = pl.ds(rows * half, rows)
    phase_out[0, here, :] = jnp.cos(edge_angle)
    phase_out[1, here, :] = jnp.sin(edge_angle)


def sheared(signals, table_ref, twist_ref, shift_cos, shift_sin, edge_ref):
    groups, width = signals[0].shape
    half = groups // 2
    edges = edge_ref.shape[0]
    size = half * len(signals)
    across, back = table_ref[:groups, : 3 * groups], table_ref[groups : 2 * groups, : 3 * groups]
    start = 2 * groups
    along_high = table_ref[start : start + 2 * width, :]
    along = jnp.concatenate([along_high, along_high, table_ref[start + 2 * width :, :]], axis=0)
    twist_cos, twist_sin = twist_ref[0, :half, :], twist_ref[1, :half, :]
    edge_cos, edge_sin = twist_ref[0, half : half + 1, :], twist_ref[1, half : half + 1, :]
    first = lax.broadcasted_iota(jnp.int32, (half, width), 0) == 0

    def stacked(blocks):
        high, low = split(jnp.concatenate(blocks, axis=1))
        return jnp.concatenate([high, low, high], axis=0)

    def transformed(value):
        high, low = split(value)
        return dot(jnp.concatenate([high, low, high], axis=1), along)

    signal = dot(across, stacked(signals))
    blocks = []
    edge_ref[...] = jnp.zeros_like(edge_ref)
    for row in range(len(signals)):
        here = slice(row * width, (row + 1) * width)
        real, imag = signal[:half, here], signal[half:, here]
        edge_ref[pl.ds(row, 1), :] = imag[:1, :]
        imag = jnp.where(first, 0.0, imag)
        blocks.append(
            jnp.concatenate([real * twist_cos + imag * twist_sin, imag * twist_cos - real * twist_sin], axis=1)
        )
    edge = edge_ref[...]
    edge = jnp.concatenate([edge * edge_cos, -edge * edge_sin], axis=1)
    spectrum = transformed(jnp.concatenate([*blocks, edge], axis=0))
    real, imag = spectrum[:, :width], spectrum[:, width:]
    spectrum = jnp.concatenate([real * shift_cos + imag * shift_sin, real * shift_sin - imag * shift_cos], axis=1)
    spectrum = transformed(spectrum)
    edge = spectrum[size:, :]
    edge_ref[...] = edge[:, :width] * edge_cos + edge[:, width:] * edge_sin
    blocks = []
    for row in range(len(signals)):
        here = slice(row * half, (row + 1) * half)
        real, imag = spectrum[here, :width], spectrum[here, width:]
        edge = jnp.broadcast_to(edge_ref[pl.ds(row, 1), :], (half, width))
        parts = [real * twist_cos + imag * twist_sin, jnp.where(first, edge, real * twist_sin - imag * twist_cos)]
        blocks.append(jnp.concatenate(parts, axis=0))
    return dot(back, stacked(blocks))


def quad_place(position, groups):
    return (position & 1) + 2 * (position // (groups // 4) & 1)


def edge_kernel(position_ref, cells_ref, keep_out, give_out, tiles, sems):
    sets, row_count, width = cells_ref.shape
    depth = tiles.shape[2]
    loads = []
    for side, start in enumerate((row_count - depth, 0)):
        for field in range(sets):
            source = cells_ref.at[field, pl.ds(start, depth)]
            loads.append(pltpu.make_async_copy(source, tiles.at[side, field], sems.at[side, field]))
            loads[-1].start()
    for load in loads:
        load.wait()
    is_odd = position_ref[0] & 1 == 1
    last = [tiles[0, field, depth - 1 :, :] for field in range(sets)]
    first = [tiles[1, field, :1, :] for field in range(sets)]
    keep = [jnp.where(is_odd, theirs, ours) for ours, theirs in zip(last, first, strict=True)]
    keep_out[...] = jnp.concatenate(keep, axis=0)
    give_out[...] = jnp.concatenate([jnp.where(is_odd, ours, theirs) for ours, theirs in zip(last, first, strict=True)], axis=0)


def shift_kernel(position_ref, whole_ref, frac_ref, _, out_ref):
    is_first = position_ref[0] & 1 == 1
    last = whole_ref.shape[1] - 1
    for place, ref in enumerate((whole_ref, frac_ref)):
        shift = jnp.where(is_first, ref[:, :1].astype(jnp.float32), ref[:, last:].astype(jnp.float32))
        out_ref[pl.ds(place, 1), :] = jnp.broadcast_to(shift, (1, out_ref.shape[1]))


def join_kernel(position_ref, shift_ref, keep_ref, got_ref, near_out, far_out, *, groups):
    is_second = quad_place(position_ref[0], groups) >= 2
    fields = [jnp.concatenate([ref[field : field + 1, :] for ref in (keep_ref, got_ref)], axis=0) for field in range(2)]
    near = jnp.where(is_second, fields[1], fields[0])
    near_out[...] = jnp.concatenate([near, shift_ref[...]], axis=0)
    far_out[...] = jnp.where(is_second, fields[0], fields[1])


def halo_kernel(position_ref, block_ref, near_ref, far_ref, phase_out, halo_out, *, groups, rows, blocks):
    is_odd = position_ref[0] & 1 == 1
    is_end = jnp.where(is_odd, block_ref[0] == blocks - 1, block_ref[0] == 0)
    near, far = [
        jnp.where(is_odd, jnp.concatenate([ref[1:2, :], ref[:1, :]], axis=0), ref[:2, :]) for ref in (near_ref, far_ref)
    ]
    is_second = quad_place(position_ref[0], groups) >= 2
    cells = jnp.where(is_second, jnp.concatenate([far, near], axis=0), jnp.concatenate([near, far], axis=0))
    halo_out[...] = jnp.where(is_end, 0.0, cells)
    whole, frac = near_ref[2:3, :].astype(jnp.int32), near_ref[3:4, :]
    width = phase_out.shape[2]
    half = groups // 2
    shape = (half, width)
    low = lax.broadcasted_iota(jnp.int32, shape, 0)
    column = lax.broadcasted_iota(jnp.int32, shape, 1)
    signed = low + groups * jnp.where(column < width // 2, column, column - width)
    edge = lax.broadcasted_iota(jnp.int32, (rows, width), 1)
    edge = half + groups * jnp.where(edge < width // 2, edge, edge - width)
    angle, edge_angle = [phase_angle(place, whole, frac, groups * width) for place in (signed, edge)]
    for part, wave in enumerate((jnp.cos, jnp.sin)):
        phase_out[part, pl.ds(0, half), :] = wave(angle)
        phase_out[part, pl.ds(half, rows), :] = wave(edge_angle)


def shear_kernel(
    position_ref, signal_ref, phase_ref, halo_ref, halo_phase_ref, table_ref, twist_ref, out_ref, edge_ref,
    *, groups, rows,
):
    pitch = rows + 1
    half = groups // 2
    signals = [signal_ref[pl.ds(row, groups, stride=rows), :] for row in range(rows)]
    width = signals[0].shape[1]
    first, step = THERE
    group = (first + step * lax.broadcasted_iota(jnp.int32, (groups, width), 0)) & (groups - 1)
    far = groups // 4
    base = position_ref[0] & groups - 1 - 1 - far
    halo = jnp.zeros((groups, width), jnp.float32)
    for place in range(QUAD):
        halo = jnp.where(group == base + place % 2 + place // 2 * far, halo_ref[place : place + 1, :], halo)
    signals.append(halo)
    shifts = []
    for part in range(2):
        ours, theirs = phase_ref[part], halo_phase_ref[part]
        cut, halo_cut = rows * half, half
        shifts.append(jnp.concatenate([ours[:cut], theirs[:halo_cut], ours[cut:], theirs[halo_cut:]], axis=0))
    signal = sheared(signals, table_ref, twist_ref, *shifts, edge_ref)
    for row in range(pitch):
        out_ref[pl.ds(row, groups, stride=pitch), :] = signal[:, row * width : (row + 1) * width]


def derivative_kernel(
    cells_ref, matrix_ref, remapped_out, radial_out, remapped, radial, sems, *, groups, rows
):
    field_count, row_count, width = remapped.shape
    pitch = cells_ref.shape[0] // groups
    parts = row_count // rows
    there, back = listed(THERE, groups), listed(BACK, groups)
    for place, group in enumerate(back):
        part = there.index(group)
        here = pl.ds(part % parts * rows, rows)
        remapped[part // parts, here, :] = cells_ref[pl.ds(place * pitch, rows), :]
    stores = [pltpu.make_async_copy(remapped, remapped_out, sems.at[field_count])]
    stores[0].start()

    shares = cells_ref[pl.ds(rows, groups, stride=pitch), :]
    first, step = BACK
    group = (first + step * lax.broadcasted_iota(jnp.int32, (groups, width), 0)) & (groups - 1)
    taken = quad_place(group, groups)

    def total(place):
        return jnp.sum(jnp.where(taken == place, shares, 0.0), axis=0, keepdims=True)

    before, after = [[total(2 * field + side) for field in range(field_count)] for side in range(2)]

    row = lax.broadcasted_iota(jnp.int32, (row_count, width), 0)
    for field in range(field_count):
        cells = remapped[field]
        above = jnp.where(row == 0, 0.0, pltpu.roll(cells, 1, 0))
        below = jnp.where(row == row_count - 1, 0.0, pltpu.roll(cells, row_count - 1, 0))
        high, low = split(below - above)
        for start in range(0, row_count, BLOCK):
            here = slice(start, start + BLOCK)
            matrix = (matrix_ref[:BLOCK, here], matrix_ref[BLOCK:, here])
            result = dot3(matrix, (high[here], low[here]))
            if start == 0:
                result -= (matrix[0][:, :1].astype(jnp.float32) + matrix[1][:, :1].astype(jnp.float32)) * before[field]
            if start == row_count - BLOCK:
                result += (matrix[0][:, -1:].astype(jnp.float32) + matrix[1][:, -1:].astype(jnp.float32)) * after[field]
            radial[field, here, :] = result
        stores.append(pltpu.make_async_copy(radial.at[field], radial_out.at[field], sems.at[field]))
        stores[-1].start()
    for store in stores:
        store.wait()


def on_device(fields, whole_shift, frac_shift, inv_spacing):
    groups = lax.axis_size("az")
    blocks = lax.axis_size("rad")
    column = lax.axis_index("az").astype(jnp.int32).reshape(1)
    part = (column - THERE[0]) * pow(THERE[1], -1, groups) & (groups - 1)
    block = lax.axis_index("rad").astype(jnp.int32).reshape(1)
    field_count, plane_count, row_count, width = fields.shape
    sets = field_count * plane_count
    rows = sets * row_count // groups
    half = groups // 2
    table = fourier_tables(groups, width)
    shifts = [row.reshape(1, row_count) for row in (whole_shift, frac_shift, inv_spacing)]
    float_of = functools.partial(jax.ShapeDtypeStruct, dtype=jnp.float32)

    signal = lax.all_to_all(
        fields.reshape(groups, rows, width), "az", 0, 0, axis_index_groups=[listed(THERE, groups)], tiled=True
    )
    table, twist, phases, matrix = pl.pallas_call(
        functools.partial(prepare_kernel, groups=groups, rows=rows),
        out_shape=(
            jax.ShapeDtypeStruct(table.shape, jnp.bfloat16),
            float_of((2, half + rows, width)),
            float_of((2, (half + 1) * rows, width)),
            jax.ShapeDtypeStruct((2 * BLOCK, row_count), jnp.bfloat16),
        ),
        in_specs=[SMEM] + [VMEM] * 5,
        out_specs=(VMEM,) * 4,
        compiler_params=PARAMS,
        cost_estimate=pl.CostEstimate(flops=10**9, transcendentals=10**5, bytes_accessed=2**21),
    )(
        part,
        *shifts,
        jnp.asarray(compact_inverse(BLOCK)),
        jnp.asarray(table),
    )
    planes = fields.reshape(sets, row_count, width)
    keep, give = pl.pallas_call(
        edge_kernel,
        out_shape=(float_of((sets, width)),) * 2,
        in_specs=[SMEM, HBM],
        out_specs=(VMEM,) * 2,
        scratch_shapes=[pltpu.VMEM((2, sets, 8, width), jnp.float32), pltpu.SemaphoreType.DMA((2, sets))],
        compiler_params=PARAMS,
    )(column, planes)
    got = lax.ppermute(give, "az", [(i, i ^ 1) for i in range(groups)])
    shift = pl.pallas_call(
        shift_kernel,
        out_shape=float_of((2, width)),
        in_specs=[SMEM] + [VMEM] * 3,
        out_specs=VMEM,
        compiler_params=PARAMS,
        cost_estimate=pl.CostEstimate(flops=10**8, transcendentals=0, bytes_accessed=2**20),
    )(column, *shifts)
    near, far = pl.pallas_call(
        functools.partial(join_kernel, groups=groups),
        out_shape=(float_of((4, width)), float_of((2, width))),
        in_specs=[SMEM] + [VMEM] * 3,
        out_specs=(VMEM,) * 2,
        compiler_params=PARAMS,
    )(column, shift, keep, got)
    turns = []
    for place in range(blocks * groups):
        step = -groups if place % 2 else groups
        turns.append((place, place + step if 0 <= place + step < blocks * groups else place ^ 1))
    near = lax.ppermute(near, ("rad", "az"), turns)
    far = lax.ppermute(far, ("rad", "az"), [(place, other ^ groups // 4) for place, other in turns])
    halo_phases, halo = pl.pallas_call(
        functools.partial(halo_kernel, groups=groups, rows=rows, blocks=blocks),
        out_shape=(float_of((2, half + rows, width)), float_of((QUAD, width))),
        in_specs=[SMEM] * 2 + [VMEM] * 2,
        out_specs=(VMEM,) * 2,
        compiler_params=PARAMS,
        cost_estimate=pl.CostEstimate(flops=10**8, transcendentals=10**4, bytes_accessed=2**18),
    )(column, block, near, far)
    pitch = rows + 1
    signal = pl.pallas_call(
        functools.partial(shear_kernel, groups=groups, rows=rows),
        out_shape=float_of((groups * pitch, width)),
        in_specs=[SMEM] + [VMEM] * 6,
        out_specs=VMEM,
        scratch_shapes=[pltpu.VMEM((2 * rows, width), jnp.float32)],
        compiler_params=PARAMS,
        cost_estimate=pl.CostEstimate(flops=10**9, transcendentals=0, bytes_accessed=2**21),
    )(column, signal.reshape(groups * rows, width), phases, halo, halo_phases, table, twist)
    signal = signal.reshape(groups, pitch, 1, width)
    signal = lax.all_to_all(signal, "az", 0, 0, axis_index_groups=[listed(BACK, groups)], tiled=True)
    signal = signal.reshape(groups * pitch, width)
    whole_shape = (sets, row_count, width)
    remapped, radial = pl.pallas_call(
        functools.partial(derivative_kernel, groups=groups, rows=rows),
        out_shape=(float_of(whole_shape), float_of(whole_shape)),
        in_specs=[VMEM] * 2,
        out_specs=(HBM, HBM),
        scratch_shapes=[
            pltpu.VMEM(whole_shape, jnp.float32),
            pltpu.VMEM(whole_shape, jnp.float32),
            pltpu.SemaphoreType.DMA((sets + 1,)),
        ],
        compiler_params=PARAMS,
    )(signal, matrix)
    return remapped.reshape(fields.shape), radial.reshape(fields.shape)


def solution(mesh):
    return jax.shard_map(
        on_device,
        mesh=mesh,
        in_specs=(P(None, None, "rad", "az"), P("rad"), P("rad"), P("rad")),
        out_specs=(P(None, None, "rad", "az"), P(None, None, "rad", "az")),
        check_vma=False,
    )
```

```python
import functools
import math

import jax
import jax.numpy as jnp
import numpy as np
from jax import lax
from jax.experimental import pallas as pl
from jax.experimental.pallas import tpu as pltpu
from jax.sharding import PartitionSpec as P

BLOCK = 128
QUAD = 4
THERE = (43, 5)
BACK = (43, 59)
VMEM = pl.BlockSpec(memory_space=pltpu.VMEM)
SMEM = pl.BlockSpec(memory_space=pltpu.SMEM)
HBM = pl.BlockSpec(memory_space=pltpu.HBM)
PARAMS = pltpu.CompilerParams(vmem_limit_bytes=24 * 2**20)


def compact_inverse(size):
    identity = np.eye(size)
    offdiag = 0.25 * (np.eye(size, k=1) + np.eye(size, k=-1))
    inverse = identity - offdiag
    power = offdiag
    for _ in range(5):
        power = power @ power
        inverse = inverse @ (identity + power)
    return inverse.astype(np.float32)


def halves(table):
    high = np.asarray(table, np.float32).astype(jnp.bfloat16)
    low = (np.asarray(table, np.float32) - high.astype(np.float32)).astype(jnp.bfloat16)
    return high, low


def split(value):
    high = value.astype(jnp.bfloat16)
    return high, (value - high.astype(jnp.float32)).astype(jnp.bfloat16)


def dot(left, right):
    return jnp.dot(left, right, preferred_element_type=jnp.float32)


def dot3(left, right):
    return dot(left[0], right[0]) + (dot(left[0], right[1]) + dot(left[1], right[0]))


def listed(order, groups):
    first, step = order
    return [(first + step * place) % groups for place in range(groups)]


def fourier_tables(groups, width):
    half = groups // 2
    low = np.arange(half + 1)
    column = np.arange(width)
    across = 2 * np.pi * (low[:, None] * np.arange(groups)[None, :] % groups) / groups
    cosine, sine = np.cos(across), np.sin(across)
    forward = np.concatenate([cosine, -sine[1:half]])
    inverse = np.concatenate([cosine[:1], 2 * cosine[1:half], cosine[half:], -2 * sine[1:half]]).T / (groups * width)
    across = []
    for table in (forward[:, listed(THERE, groups)], inverse[listed(BACK, groups)]):
        high, low = halves(table)
        across.append(np.pad(np.concatenate([high, high, low], axis=1), ((0, 0), (0, 2 * width - 3 * groups))))
    grid = 2 * np.pi * (column[:, None] * column[None, :] % width) / width
    cosine, sine = np.cos(grid), np.sin(grid)
    along = halves(np.block([[cosine, -sine], [sine, cosine]]))
    return np.concatenate([*across, *along])


def phase_angle(signed, whole, frac, total):
    turns = ((signed * whole) & (total - 1)).astype(jnp.float32) + signed.astype(jnp.float32) * frac
    return (2.0 * math.pi / total) * turns


def prepare_kernel(
    part_ref, whole_ref, frac_ref, spacing_ref, compact_ref, table_ref,
    table_out, twist_out, phase_out, matrix_out,
    *, groups, rows,
):
    table_out[...] = table_ref[...]
    scale = 0.75 * spacing_ref[...]
    for start in range(0, scale.shape[1], BLOCK):
        here = slice(start, start + BLOCK)
        matrix_out[:BLOCK, here], matrix_out[BLOCK:, here] = split(compact_ref[...] * scale[:, here])
    half = groups // 2
    width = twist_out.shape[2]
    total = groups * width
    row_count = whole_ref.shape[1]
    shape = (half, width)
    low = lax.broadcasted_iota(jnp.int32, shape, 0)
    column = lax.broadcasted_iota(jnp.int32, shape, 1)
    angle = (2.0 * math.pi / total) * (low * column).astype(jnp.float32)
    twist_out[0, :half, :] = jnp.cos(angle)
    twist_out[1, :half, :] = jnp.sin(angle)
    edge = lax.broadcasted_iota(jnp.int32, (rows, width), 1)
    angle = (2.0 * math.pi / total) * (half * edge).astype(jnp.float32)
    twist_out[0, half:, :] = jnp.cos(angle)
    twist_out[1, half:, :] = jnp.sin(angle)
    signed = low + groups * jnp.where(column < width // 2, column, column - width)
    edge = half + groups * jnp.where(edge < width // 2, edge, edge - width)
    edge_row = lax.broadcasted_iota(jnp.int32, (rows, width), 0)
    lane = lax.broadcasted_iota(jnp.int32, (rows, row_count), 1)
    first = lax.rem(part_ref[0] * rows, row_count)
    own = lane == first + lax.broadcasted_iota(jnp.int32, (rows, row_count), 0)
    wholes = jnp.sum(jnp.where(own, whole_ref[...].astype(jnp.float32), 0.0), axis=1, keepdims=True).astype(jnp.int32)
    fracs = jnp.sum(jnp.where(own, frac_ref[...], 0.0), axis=1, keepdims=True)
    edge_angle = jnp.zeros((rows, width), jnp.float32)
    for row in range(rows):
        whole, frac = wholes[row : row + 1], fracs[row : row + 1]
        angle = phase_angle(signed, whole, frac, total)
        here = pl.ds(row * half, half)
        phase_out[0, here, :] = jnp.cos(angle)
        phase_out[1, here, :] = jnp.sin(angle)
        edge_angle = jnp.where(edge_row == row, phase_angle(edge, whole, frac, total), edge_angle)
    here = pl.ds(rows * half, rows)
    phase_out[0, here, :] = jnp.cos(edge_angle)
    phase_out[1, here, :] = jnp.sin(edge_angle)


def sheared(signals, table_ref, twist_ref, shift_cos, shift_sin, edge_ref):
    groups, width = signals[0].shape
    half = groups // 2
    edges = edge_ref.shape[0]
    size = half * len(signals)
    across, back = table_ref[:groups, : 3 * groups], table_ref[groups : 2 * groups, : 3 * groups]
    start = 2 * groups
    along_high = table_ref[start : start + 2 * width, :]
    along = jnp.concatenate([along_high, along_high, table_ref[start + 2 * width :, :]], axis=0)
    twist_cos, twist_sin = twist_ref[0, :half, :], twist_ref[1, :half, :]
    edge_cos, edge_sin = twist_ref[0, half : half + 1, :], twist_ref[1, half : half + 1, :]
    first = lax.broadcasted_iota(jnp.int32, (half, width), 0) == 0

    def stacked(blocks):
        high, low = split(jnp.concatenate(blocks, axis=1))
        return jnp.concatenate([high, low, high], axis=0)

    def transformed(value):
        high, low = split(value)
        return dot(jnp.concatenate([high, low, high], axis=1), along)

    signal = dot(across, stacked(signals))
    blocks = []
    edge_ref[...] = jnp.zeros_like(edge_ref)
    for row in range(len(signals)):
        here = slice(row * width, (row + 1) * width)
        real, imag = signal[:half, here], signal[half:, here]
        edge_ref[pl.ds(row, 1), :] = imag[:1, :]
        imag = jnp.where(first, 0.0, imag)
        blocks.append(
            jnp.concatenate([real * twist_cos + imag * twist_sin, imag * twist_cos - real * twist_sin], axis=1)
        )
    edge = edge_ref[...]
    edge = jnp.concatenate([edge * edge_cos, -edge * edge_sin], axis=1)
    spectrum = transformed(jnp.concatenate([*blocks, edge], axis=0))
    real, imag = spectrum[:, :width], spectrum[:, width:]
    spectrum = jnp.concatenate([real * shift_cos + imag * shift_sin, real * shift_sin - imag * shift_cos], axis=1)
    spectrum = transformed(spectrum)
    edge = spectrum[size:, :]
    edge_ref[...] = edge[:, :width] * edge_cos + edge[:, width:] * edge_sin
    blocks = []
    for row in range(len(signals)):
        here = slice(row * half, (row + 1) * half)
        real, imag = spectrum[here, :width], spectrum[here, width:]
        edge = jnp.broadcast_to(edge_ref[pl.ds(row, 1), :], (half, width))
        parts = [real * twist_cos + imag * twist_sin, jnp.where(first, edge, real * twist_sin - imag * twist_cos)]
        blocks.append(jnp.concatenate(parts, axis=0))
    return dot(back, stacked(blocks))


def quad_place(position, groups):
    return (position & 1) + 2 * (position // (groups // 4) & 1)


def edge_kernel(position_ref, cells_ref, keep_out, give_out, tiles, sems):
    sets, row_count, width = cells_ref.shape
    depth = tiles.shape[2]
    loads = []
    for side, start in enumerate((row_count - depth, 0)):
        for field in range(sets):
            source = cells_ref.at[field, pl.ds(start, depth)]
            loads.append(pltpu.make_async_copy(source, tiles.at[side, field], sems.at[side, field]))
            loads[-1].start()
    for load in loads:
        load.wait()
    is_odd = position_ref[0] & 1 == 1
    last = [tiles[0, field, depth - 1 :, :] for field in range(sets)]
    first = [tiles[1, field, :1, :] for field in range(sets)]
    keep = [jnp.where(is_odd, theirs, ours) for ours, theirs in zip(last, first, strict=True)]
    keep_out[...] = jnp.concatenate(keep, axis=0)
    give_out[...] = jnp.concatenate([jnp.where(is_odd, ours, theirs) for ours, theirs in zip(last, first, strict=True)], axis=0)


def shift_kernel(position_ref, whole_ref, frac_ref, _, out_ref):
    is_first = position_ref[0] & 1 == 1
    last = whole_ref.shape[1] - 1
    for place, ref in enumerate((whole_ref, frac_ref)):
        shift = jnp.where(is_first, ref[:, :1].astype(jnp.float32), ref[:, last:].astype(jnp.float32))
        out_ref[pl.ds(place, 1), :] = jnp.broadcast_to(shift, (1, out_ref.shape[1]))


def join_kernel(position_ref, shift_ref, keep_ref, got_ref, near_out, far_out, *, groups):
    is_second = quad_place(position_ref[0], groups) >= 2
    fields = [jnp.concatenate([ref[field : field + 1, :] for ref in (keep_ref, got_ref)], axis=0) for field in range(2)]
    near = jnp.where(is_second, fields[1], fields[0])
    near_out[...] = jnp.concatenate([near, shift_ref[...]], axis=0)
    far_out[...] = jnp.where(is_second, fields[0], fields[1])


def halo_kernel(position_ref, block_ref, near_ref, far_ref, phase_out, halo_out, *, groups, rows, blocks):
    is_odd = position_ref[0] & 1 == 1
    is_end = jnp.where(is_odd, block_ref[0] == blocks - 1, block_ref[0] == 0)
    near, far = [
        jnp.where(is_odd, jnp.concatenate([ref[1:2, :], ref[:1, :]], axis=0), ref[:2, :]) for ref in (near_ref, far_ref)
    ]
    is_second = quad_place(position_ref[0], groups) >= 2
    cells = jnp.where(is_second, jnp.concatenate([far, near], axis=0), jnp.concatenate([near, far], axis=0))
    halo_out[...] = jnp.where(is_end, 0.0, cells)
    whole, frac = near_ref[2:3, :].astype(jnp.int32), near_ref[3:4, :]
    width = phase_out.shape[2]
    half = groups // 2
    shape = (half, width)
    low = lax.broadcasted_iota(jnp.int32, shape, 0)
    column = lax.broadcasted_iota(jnp.int32, shape, 1)
    signed = low + groups * jnp.where(column < width // 2, column, column - width)
    edge = lax.broadcasted_iota(jnp.int32, (rows, width), 1)
    edge = half + groups * jnp.where(edge < width // 2, edge, edge - width)
    angle, edge_angle = [phase_angle(place, whole, frac, groups * width) for place in (signed, edge)]
    for part, wave in enumerate((jnp.cos, jnp.sin)):
        phase_out[part, pl.ds(0, half), :] = wave(angle)
        phase_out[part, pl.ds(half, rows), :] = wave(edge_angle)


def shear_kernel(
    position_ref, signal_ref, phase_ref, halo_ref, halo_phase_ref, table_ref, twist_ref, out_ref, edge_ref,
    *, groups, rows,
):
    pitch = rows + 1
    half = groups // 2
    signals = [signal_ref[pl.ds(row, groups, stride=rows), :] for row in range(rows)]
    width = signals[0].shape[1]
    first, step = THERE
    group = (first + step * lax.broadcasted_iota(jnp.int32, (groups, width), 0)) & (groups - 1)
    far = groups // 4
    base = position_ref[0] & groups - 1 - 1 - far
    halo = jnp.zeros((groups, width), jnp.float32)
    for place in range(QUAD):
        halo = jnp.where(group == base + place % 2 + place // 2 * far, halo_ref[place : place + 1, :], halo)
    signals.append(halo)
    shifts = []
    for part in range(2):
        ours, theirs = phase_ref[part], halo_phase_ref[part]
        cut, halo_cut = rows * half, half
        shifts.append(jnp.concatenate([ours[:cut], theirs[:halo_cut], ours[cut:], theirs[halo_cut:]], axis=0))
    signal = sheared(signals, table_ref, twist_ref, *shifts, edge_ref)
    for row in range(pitch):
        out_ref[pl.ds(row, groups, stride=pitch), :] = signal[:, row * width : (row + 1) * width]


def derivative_kernel(
    cells_ref, matrix_ref, remapped_out, radial_out, remapped, radial, sems, *, groups, rows
):
    field_count, row_count, width = remapped.shape
    pitch = cells_ref.shape[0] // groups
    parts = row_count // rows
    there, back = listed(THERE, groups), listed(BACK, groups)
    stores = []

    def store(source, target):
        stores.append(pltpu.make_async_copy(source, target, sems.at[len(stores)]))
        stores[-1].start()

    for field in range(field_count):
        for part in range(parts):
            place = back.index(there[field * parts + part])
            remapped[field, pl.ds(part * rows, rows), :] = cells_ref[pl.ds(place * pitch, rows), :]
        store(remapped.at[field], remapped_out.at[field])

    shares = cells_ref[pl.ds(rows, groups, stride=pitch), :]
    first, step = BACK
    group = (first + step * lax.broadcasted_iota(jnp.int32, (groups, width), 0)) & (groups - 1)
    taken = quad_place(group, groups)

    def total(place):
        return jnp.sum(jnp.where(taken == place, shares, 0.0), axis=0, keepdims=True)

    before, after = [[total(2 * field + side) for field in range(field_count)] for side in range(2)]

    row = lax.broadcasted_iota(jnp.int32, (row_count, width), 0)
    for field in range(field_count):
        cells = remapped[field]
        above = jnp.where(row == 0, 0.0, pltpu.roll(cells, 1, 0))
        below = jnp.where(row == row_count - 1, 0.0, pltpu.roll(cells, row_count - 1, 0))
        high, low = split(below - above)
        for start in range(0, row_count, BLOCK):
            here = slice(start, start + BLOCK)
            matrix = (matrix_ref[:BLOCK, here], matrix_ref[BLOCK:, here])
            result = dot3(matrix, (high[here], low[here]))
            if start == 0:
                result -= (matrix[0][:, :1].astype(jnp.float32) + matrix[1][:, :1].astype(jnp.float32)) * before[field]
            if start == row_count - BLOCK:
                result += (matrix[0][:, -1:].astype(jnp.float32) + matrix[1][:, -1:].astype(jnp.float32)) * after[field]
            radial[field, here, :] = result
            spot = (field, pl.ds(start, BLOCK))
            store(radial.at[spot], radial_out.at[spot])
    for copy in stores:
        copy.wait()


def on_device(fields, whole_shift, frac_shift, inv_spacing):
    groups = lax.axis_size("az")
    blocks = lax.axis_size("rad")
    column = lax.axis_index("az").astype(jnp.int32).reshape(1)
    part = (column - THERE[0]) * pow(THERE[1], -1, groups) & (groups - 1)
    block = lax.axis_index("rad").astype(jnp.int32).reshape(1)
    field_count, plane_count, row_count, width = fields.shape
    sets = field_count * plane_count
    rows = sets * row_count // groups
    half = groups // 2
    table = fourier_tables(groups, width)
    shifts = [row.reshape(1, row_count) for row in (whole_shift, frac_shift, inv_spacing)]
    float_of = functools.partial(jax.ShapeDtypeStruct, dtype=jnp.float32)

    signal = lax.all_to_all(
        fields.reshape(groups, rows, width), "az", 0, 0, axis_index_groups=[listed(THERE, groups)], tiled=True
    )
    table, twist, phases, matrix = pl.pallas_call(
        functools.partial(prepare_kernel, groups=groups, rows=rows),
        out_shape=(
            jax.ShapeDtypeStruct(table.shape, jnp.bfloat16),
            float_of((2, half + rows, width)),
            float_of((2, (half + 1) * rows, width)),
            jax.ShapeDtypeStruct((2 * BLOCK, row_count), jnp.bfloat16),
        ),
        in_specs=[SMEM] + [VMEM] * 5,
        out_specs=(VMEM,) * 4,
        compiler_params=PARAMS,
        cost_estimate=pl.CostEstimate(flops=10**9, transcendentals=10**5, bytes_accessed=2**21),
    )(
        part,
        *shifts,
        jnp.asarray(compact_inverse(BLOCK)),
        jnp.asarray(table),
    )
    planes = fields.reshape(sets, row_count, width)
    keep, give = pl.pallas_call(
        edge_kernel,
        out_shape=(float_of((sets, width)),) * 2,
        in_specs=[SMEM, HBM],
        out_specs=(VMEM,) * 2,
        scratch_shapes=[pltpu.VMEM((2, sets, 8, width), jnp.float32), pltpu.SemaphoreType.DMA((2, sets))],
        compiler_params=PARAMS,
    )(column, planes)
    got = lax.ppermute(give, "az", [(i, i ^ 1) for i in range(groups)])
    shift = pl.pallas_call(
        shift_kernel,
        out_shape=float_of((2, width)),
        in_specs=[SMEM] + [VMEM] * 3,
        out_specs=VMEM,
        compiler_params=PARAMS,
        cost_estimate=pl.CostEstimate(flops=10**8, transcendentals=0, bytes_accessed=2**20),
    )(column, *shifts)
    near, far = pl.pallas_call(
        functools.partial(join_kernel, groups=groups),
        out_shape=(float_of((4, width)), float_of((2, width))),
        in_specs=[SMEM] + [VMEM] * 3,
        out_specs=(VMEM,) * 2,
        compiler_params=PARAMS,
    )(column, shift, keep, got)
    turns = []
    for place in range(blocks * groups):
        step = -groups if place % 2 else groups
        turns.append((place, place + step if 0 <= place + step < blocks * groups else place ^ 1))
    near = lax.ppermute(near, ("rad", "az"), turns)
    far = lax.ppermute(far, ("rad", "az"), [(place, other ^ groups // 4) for place, other in turns])
    halo_phases, halo = pl.pallas_call(
        functools.partial(halo_kernel, groups=groups, rows=rows, blocks=blocks),
        out_shape=(float_of((2, half + rows, width)), float_of((QUAD, width))),
        in_specs=[SMEM] * 2 + [VMEM] * 2,
        out_specs=(VMEM,) * 2,
        compiler_params=PARAMS,
        cost_estimate=pl.CostEstimate(flops=10**8, transcendentals=10**4, bytes_accessed=2**18),
    )(column, block, near, far)
    pitch = rows + 1
    signal = pl.pallas_call(
        functools.partial(shear_kernel, groups=groups, rows=rows),
        out_shape=float_of((groups * pitch, width)),
        in_specs=[SMEM] + [VMEM] * 6,
        out_specs=VMEM,
        scratch_shapes=[pltpu.VMEM((2 * rows, width), jnp.float32)],
        compiler_params=PARAMS,
        cost_estimate=pl.CostEstimate(flops=10**9, transcendentals=0, bytes_accessed=2**21),
    )(column, signal.reshape(groups * rows, width), phases, halo, halo_phases, table, twist)
    signal = signal.reshape(groups, pitch, 1, width)
    signal = lax.all_to_all(signal, "az", 0, 0, axis_index_groups=[listed(BACK, groups)], tiled=True)
    signal = signal.reshape(groups * pitch, width)
    whole_shape = (sets, row_count, width)
    remapped, radial = pl.pallas_call(
        functools.partial(derivative_kernel, groups=groups, rows=rows),
        out_shape=(float_of(whole_shape), float_of(whole_shape)),
        in_specs=[VMEM] * 2,
        out_specs=(HBM, HBM),
        scratch_shapes=[
            pltpu.VMEM(whole_shape, jnp.float32),
            pltpu.VMEM(whole_shape, jnp.float32),
            pltpu.SemaphoreType.DMA((sets + sets * row_count // BLOCK,)),
        ],
        compiler_params=PARAMS,
    )(signal, matrix)
    return remapped.reshape(fields.shape), radial.reshape(fields.shape)


def solution(mesh):
    return jax.shard_map(
        on_device,
        mesh=mesh,
        in_specs=(P(None, None, "rad", "az"), P("rad"), P("rad"), P("rad")),
        out_specs=(P(None, None, "rad", "az"), P(None, None, "rad", "az")),
        check_vma=False,
    )
```

```python
import functools
import math

import jax
import jax.numpy as jnp
import numpy as np
from jax import lax
from jax.experimental import pallas as pl
from jax.experimental.pallas import tpu as pltpu
from jax.sharding import PartitionSpec as P

BLOCK = 128
QUAD = 4
THERE = (43, 5)
BACK = (41, 59)
VMEM = pl.BlockSpec(memory_space=pltpu.VMEM)
SMEM = pl.BlockSpec(memory_space=pltpu.SMEM)
HBM = pl.BlockSpec(memory_space=pltpu.HBM)
PARAMS = pltpu.CompilerParams(vmem_limit_bytes=24 * 2**20)


def compact_inverse(size):
    identity = np.eye(size)
    offdiag = 0.25 * (np.eye(size, k=1) + np.eye(size, k=-1))
    inverse = identity - offdiag
    power = offdiag
    for _ in range(5):
        power = power @ power
        inverse = inverse @ (identity + power)
    return inverse.astype(np.float32)


def halves(table):
    high = np.asarray(table, np.float32).astype(jnp.bfloat16)
    low = (np.asarray(table, np.float32) - high.astype(np.float32)).astype(jnp.bfloat16)
    return high, low


def split(value):
    high = value.astype(jnp.bfloat16)
    return high, (value - high.astype(jnp.float32)).astype(jnp.bfloat16)


def dot(left, right):
    return jnp.dot(left, right, preferred_element_type=jnp.float32)


def dot3(left, right):
    return dot(left[0], right[0]) + (dot(left[0], right[1]) + dot(left[1], right[0]))


def listed(order, groups):
    first, step = order
    return [(first + step * place) % groups for place in range(groups)]


def fourier_tables(groups, width):
    half = groups // 2
    low = np.arange(half + 1)
    column = np.arange(width)
    across = 2 * np.pi * (low[:, None] * np.arange(groups)[None, :] % groups) / groups
    cosine, sine = np.cos(across), np.sin(across)
    forward = np.concatenate([cosine, -sine[1:half]])
    inverse = np.concatenate([cosine[:1], 2 * cosine[1:half], cosine[half:], -2 * sine[1:half]]).T / (groups * width)
    across = []
    for table in (forward[:, listed(THERE, groups)], inverse[listed(BACK, groups)]):
        high, low = halves(table)
        across.append(np.pad(np.concatenate([high, high, low], axis=1), ((0, 0), (0, 2 * width - 3 * groups))))
    grid = 2 * np.pi * (column[:, None] * column[None, :] % width) / width
    cosine, sine = np.cos(grid), np.sin(grid)
    along = halves(np.block([[cosine, -sine], [sine, cosine]]))
    return np.concatenate([*across, *along])


def phase_angle(signed, whole, frac, total):
    turns = ((signed * whole) & (total - 1)).astype(jnp.float32) + signed.astype(jnp.float32) * frac
    return (2.0 * math.pi / total) * turns


def prepare_kernel(
    part_ref, whole_ref, frac_ref, spacing_ref, compact_ref, table_ref,
    table_out, twist_out, phase_out, matrix_out,
    *, groups, rows,
):
    table_out[...] = table_ref[...]
    scale = 0.75 * spacing_ref[...]
    for start in range(0, scale.shape[1], BLOCK):
        here = slice(start, start + BLOCK)
        matrix_out[:BLOCK, here], matrix_out[BLOCK:, here] = split(compact_ref[...] * scale[:, here])
    half = groups // 2
    width = twist_out.shape[2]
    total = groups * width
    row_count = whole_ref.shape[1]
    shape = (half, width)
    low = lax.broadcasted_iota(jnp.int32, shape, 0)
    column = lax.broadcasted_iota(jnp.int32, shape, 1)
    angle = (2.0 * math.pi / total) * (low * column).astype(jnp.float32)
    twist_out[0, :half, :] = jnp.cos(angle)
    twist_out[1, :half, :] = jnp.sin(angle)
    edge = lax.broadcasted_iota(jnp.int32, (rows, width), 1)
    angle = (2.0 * math.pi / total) * (half * edge).astype(jnp.float32)
    twist_out[0, half:, :] = jnp.cos(angle)
    twist_out[1, half:, :] = jnp.sin(angle)
    signed = low + groups * jnp.where(column < width // 2, column, column - width)
    edge = half + groups * jnp.where(edge < width // 2, edge, edge - width)
    edge_row = lax.broadcasted_iota(jnp.int32, (rows, width), 0)
    lane = lax.broadcasted_iota(jnp.int32, (rows, row_count), 1)
    first = lax.rem(part_ref[0] * rows, row_count)
    own = lane == first + lax.broadcasted_iota(jnp.int32, (rows, row_count), 0)
    wholes = jnp.sum(jnp.where(own, whole_ref[...].astype(jnp.float32), 0.0), axis=1, keepdims=True).astype(jnp.int32)
    fracs = jnp.sum(jnp.where(own, frac_ref[...], 0.0), axis=1, keepdims=True)
    edge_angle = jnp.zeros((rows, width), jnp.float32)
    for row in range(rows):
        whole, frac = wholes[row : row + 1], fracs[row : row + 1]
        angle = phase_angle(signed, whole, frac, total)
        here = pl.ds(row * half, half)
        phase_out[0, here, :] = jnp.cos(angle)
        phase_out[1, here, :] = jnp.sin(angle)
        edge_angle = jnp.where(edge_row == row, phase_angle(edge, whole, frac, total), edge_angle)
    here = pl.ds(rows * half, rows)
    phase_out[0, here, :] = jnp.cos(edge_angle)
    phase_out[1, here, :] = jnp.sin(edge_angle)


def sheared(signals, table_ref, twist_ref, shift_cos, shift_sin, edge_ref):
    groups, width = signals[0].shape
    half = groups // 2
    edges = edge_ref.shape[0]
    size = half * len(signals)
    across, back = table_ref[:groups, : 3 * groups], table_ref[groups : 2 * groups, : 3 * groups]
    start = 2 * groups
    along_high = table_ref[start : start + 2 * width, :]
    along = jnp.concatenate([along_high, along_high, table_ref[start + 2 * width :, :]], axis=0)
    twist_cos, twist_sin = twist_ref[0, :half, :], twist_ref[1, :half, :]
    edge_cos, edge_sin = twist_ref[0, half : half + 1, :], twist_ref[1, half : half + 1, :]
    first = lax.broadcasted_iota(jnp.int32, (half, width), 0) == 0

    def stacked(blocks):
        high, low = split(jnp.concatenate(blocks, axis=1))
        return jnp.concatenate([high, low, high], axis=0)

    def transformed(value):
        high, low = split(value)
        return dot(jnp.concatenate([high, low, high], axis=1), along)

    signal = dot(across, stacked(signals))
    blocks = []
    edge_ref[...] = jnp.zeros_like(edge_ref)
    for row in range(len(signals)):
        here = slice(row * width, (row + 1) * width)
        real, imag = signal[:half, here], signal[half:, here]
        edge_ref[pl.ds(row, 1), :] = imag[:1, :]
        imag = jnp.where(first, 0.0, imag)
        blocks.append(
            jnp.concatenate([real * twist_cos + imag * twist_sin, imag * twist_cos - real * twist_sin], axis=1)
        )
    edge = edge_ref[...]
    edge = jnp.concatenate([edge * edge_cos, -edge * edge_sin], axis=1)
    spectrum = transformed(jnp.concatenate([*blocks, edge], axis=0))
    real, imag = spectrum[:, :width], spectrum[:, width:]
    spectrum = jnp.concatenate([real * shift_cos + imag * shift_sin, real * shift_sin - imag * shift_cos], axis=1)
    spectrum = transformed(spectrum)
    edge = spectrum[size:, :]
    edge_ref[...] = edge[:, :width] * edge_cos + edge[:, width:] * edge_sin
    blocks = []
    for row in range(len(signals)):
        here = slice(row * half, (row + 1) * half)
        real, imag = spectrum[here, :width], spectrum[here, width:]
        edge = jnp.broadcast_to(edge_ref[pl.ds(row, 1), :], (half, width))
        parts = [real * twist_cos + imag * twist_sin, jnp.where(first, edge, real * twist_sin - imag * twist_cos)]
        blocks.append(jnp.concatenate(parts, axis=0))
    return dot(back, stacked(blocks))


def quad_place(position, groups):
    return (position & 1) + 2 * (position // (groups // 4) & 1)


def edge_kernel(position_ref, cells_ref, keep_out, give_out, tiles, sems):
    sets, row_count, width = cells_ref.shape
    depth = tiles.shape[2]
    loads = []
    for side, start in enumerate((row_count - depth, 0)):
        for field in range(sets):
            source = cells_ref.at[field, pl.ds(start, depth)]
            loads.append(pltpu.make_async_copy(source, tiles.at[side, field], sems.at[side, field]))
            loads[-1].start()
    for load in loads:
        load.wait()
    is_odd = position_ref[0] & 1 == 1
    last = [tiles[0, field, depth - 1 :, :] for field in range(sets)]
    first = [tiles[1, field, :1, :] for field in range(sets)]
    keep = [jnp.where(is_odd, theirs, ours) for ours, theirs in zip(last, first, strict=True)]
    keep_out[...] = jnp.concatenate(keep, axis=0)
    give_out[...] = jnp.concatenate([jnp.where(is_odd, ours, theirs) for ours, theirs in zip(last, first, strict=True)], axis=0)


def shift_kernel(position_ref, whole_ref, frac_ref, _, out_ref):
    is_first = position_ref[0] & 1 == 1
    last = whole_ref.shape[1] - 1
    for place, ref in enumerate((whole_ref, frac_ref)):
        shift = jnp.where(is_first, ref[:, :1].astype(jnp.float32), ref[:, last:].astype(jnp.float32))
        out_ref[pl.ds(place, 1), :] = jnp.broadcast_to(shift, (1, out_ref.shape[1]))


def join_kernel(position_ref, shift_ref, keep_ref, got_ref, near_out, far_out, *, groups):
    is_second = quad_place(position_ref[0], groups) >= 2
    fields = [jnp.concatenate([ref[field : field + 1, :] for ref in (keep_ref, got_ref)], axis=0) for field in range(2)]
    near = jnp.where(is_second, fields[1], fields[0])
    near_out[...] = jnp.concatenate([near, shift_ref[...]], axis=0)
    far_out[...] = jnp.where(is_second, fields[0], fields[1])


def halo_kernel(position_ref, block_ref, near_ref, far_ref, phase_out, halo_out, *, groups, rows, blocks):
    is_odd = position_ref[0] & 1 == 1
    is_end = jnp.where(is_odd, block_ref[0] == blocks - 1, block_ref[0] == 0)
    near, far = [
        jnp.where(is_odd, jnp.concatenate([ref[1:2, :], ref[:1, :]], axis=0), ref[:2, :]) for ref in (near_ref, far_ref)
    ]
    is_second = quad_place(position_ref[0], groups) >= 2
    cells = jnp.where(is_second, jnp.concatenate([far, near], axis=0), jnp.concatenate([near, far], axis=0))
    halo_out[...] = jnp.where(is_end, 0.0, cells)
    whole, frac = near_ref[2:3, :].astype(jnp.int32), near_ref[3:4, :]
    width = phase_out.shape[2]
    half = groups // 2
    shape = (half, width)
    low = lax.broadcasted_iota(jnp.int32, shape, 0)
    column = lax.broadcasted_iota(jnp.int32, shape, 1)
    signed = low + groups * jnp.where(column < width // 2, column, column - width)
    edge = lax.broadcasted_iota(jnp.int32, (rows, width), 1)
    edge = half + groups * jnp.where(edge < width // 2, edge, edge - width)
    angle, edge_angle = [phase_angle(place, whole, frac, groups * width) for place in (signed, edge)]
    for part, wave in enumerate((jnp.cos, jnp.sin)):
        phase_out[part, pl.ds(0, half), :] = wave(angle)
        phase_out[part, pl.ds(half, rows), :] = wave(edge_angle)


def shear_kernel(
    position_ref, signal_ref, phase_ref, halo_ref, halo_phase_ref, table_ref, twist_ref, out_ref, edge_ref,
    *, groups, rows,
):
    pitch = rows + 1
    half = groups // 2
    signals = [signal_ref[pl.ds(row, groups, stride=rows), :] for row in range(rows)]
    width = signals[0].shape[1]
    first, step = THERE
    group = (first + step * lax.broadcasted_iota(jnp.int32, (groups, width), 0)) & (groups - 1)
    far = groups // 4
    base = position_ref[0] & groups - 1 - 1 - far
    halo = jnp.zeros((groups, width), jnp.float32)
    for place in range(QUAD):
        halo = jnp.where(group == base + place % 2 + place // 2 * far, halo_ref[place : place + 1, :], halo)
    signals.append(halo)
    shifts = []
    for part in range(2):
        ours, theirs = phase_ref[part], halo_phase_ref[part]
        cut, halo_cut = rows * half, half
        shifts.append(jnp.concatenate([ours[:cut], theirs[:halo_cut], ours[cut:], theirs[halo_cut:]], axis=0))
    signal = sheared(signals, table_ref, twist_ref, *shifts, edge_ref)
    for row in range(pitch):
        out_ref[pl.ds(row, groups, stride=pitch), :] = signal[:, row * width : (row + 1) * width]


def derivative_kernel(
    cells_ref, matrix_ref, remapped_out, radial_out, remapped, radial, sems, *, groups, rows
):
    field_count, row_count, width = remapped.shape
    pitch = cells_ref.shape[0] // groups
    parts = row_count // rows
    there, back = listed(THERE, groups), listed(BACK, groups)
    stores = []

    def store(source, target):
        stores.append(pltpu.make_async_copy(source, target, sems.at[len(stores)]))
        stores[-1].start()

    for field in range(field_count):
        for part in range(parts):
            place = back.index(there[field * parts + part])
            remapped[field, pl.ds(part * rows, rows), :] = cells_ref[pl.ds(place * pitch, rows), :]
        store(remapped.at[field], remapped_out.at[field])

    shares = cells_ref[pl.ds(rows, groups, stride=pitch), :]
    first, step = BACK
    group = (first + step * lax.broadcasted_iota(jnp.int32, (groups, width), 0)) & (groups - 1)
    taken = quad_place(group, groups)

    def total(place):
        return jnp.sum(jnp.where(taken == place, shares, 0.0), axis=0, keepdims=True)

    before, after = [[total(2 * field + side) for field in range(field_count)] for side in range(2)]

    row = lax.broadcasted_iota(jnp.int32, (row_count, width), 0)
    for field in range(field_count):
        cells = remapped[field]
        above = jnp.where(row == 0, 0.0, pltpu.roll(cells, 1, 0))
        below = jnp.where(row == row_count - 1, 0.0, pltpu.roll(cells, row_count - 1, 0))
        high, low = split(below - above)
        for start in range(0, row_count, BLOCK):
            here = slice(start, start + BLOCK)
            matrix = (matrix_ref[:BLOCK, here], matrix_ref[BLOCK:, here])
            result = dot3(matrix, (high[here], low[here]))
            if start == 0:
                result -= (matrix[0][:, :1].astype(jnp.float32) + matrix[1][:, :1].astype(jnp.float32)) * before[field]
            if start == row_count - BLOCK:
                result += (matrix[0][:, -1:].astype(jnp.float32) + matrix[1][:, -1:].astype(jnp.float32)) * after[field]
            radial[field, here, :] = result
            spot = (field, pl.ds(start, BLOCK))
            store(radial.at[spot], radial_out.at[spot])
    for copy in stores:
        copy.wait()


def on_device(fields, whole_shift, frac_shift, inv_spacing):
    groups = lax.axis_size("az")
    blocks = lax.axis_size("rad")
    column = lax.axis_index("az").astype(jnp.int32).reshape(1)
    part = (column - THERE[0]) * pow(THERE[1], -1, groups) & (groups - 1)
    block = lax.axis_index("rad").astype(jnp.int32).reshape(1)
    field_count, plane_count, row_count, width = fields.shape
    sets = field_count * plane_count
    rows = sets * row_count // groups
    half = groups // 2
    table = fourier_tables(groups, width)
    shifts = [row.reshape(1, row_count) for row in (whole_shift, frac_shift, inv_spacing)]
    float_of = functools.partial(jax.ShapeDtypeStruct, dtype=jnp.float32)

    signal = lax.all_to_all(
        fields.reshape(groups, rows, width), "az", 0, 0, axis_index_groups=[listed(THERE, groups)], tiled=True
    )
    table, twist, phases, matrix = pl.pallas_call(
        functools.partial(prepare_kernel, groups=groups, rows=rows),
        out_shape=(
            jax.ShapeDtypeStruct(table.shape, jnp.bfloat16),
            float_of((2, half + rows, width)),
            float_of((2, (half + 1) * rows, width)),
            jax.ShapeDtypeStruct((2 * BLOCK, row_count), jnp.bfloat16),
        ),
        in_specs=[SMEM] + [VMEM] * 5,
        out_specs=(VMEM,) * 4,
        compiler_params=PARAMS,
        cost_estimate=pl.CostEstimate(flops=10**9, transcendentals=10**5, bytes_accessed=2**21),
    )(
        part,
        *shifts,
        jnp.asarray(compact_inverse(BLOCK)),
        jnp.asarray(table),
    )
    planes = fields.reshape(sets, row_count, width)
    keep, give = pl.pallas_call(
        edge_kernel,
        out_shape=(float_of((sets, width)),) * 2,
        in_specs=[SMEM, HBM],
        out_specs=(VMEM,) * 2,
        scratch_shapes=[pltpu.VMEM((2, sets, 8, width), jnp.float32), pltpu.SemaphoreType.DMA((2, sets))],
        compiler_params=PARAMS,
    )(column, planes)
    got = lax.ppermute(give, "az", [(i, i ^ 1) for i in range(groups)])
    shift = pl.pallas_call(
        shift_kernel,
        out_shape=float_of((2, width)),
        in_specs=[SMEM] + [VMEM] * 3,
        out_specs=VMEM,
        compiler_params=PARAMS,
        cost_estimate=pl.CostEstimate(flops=10**8, transcendentals=0, bytes_accessed=2**20),
    )(column, *shifts)
    near, far = pl.pallas_call(
        functools.partial(join_kernel, groups=groups),
        out_shape=(float_of((4, width)), float_of((2, width))),
        in_specs=[SMEM] + [VMEM] * 3,
        out_specs=(VMEM,) * 2,
        compiler_params=PARAMS,
    )(column, shift, keep, got)
    turns = []
    for place in range(blocks * groups):
        step = -groups if place % 2 else groups
        turns.append((place, place + step if 0 <= place + step < blocks * groups else place ^ 1))
    near = lax.ppermute(near, ("rad", "az"), turns)
    far = lax.ppermute(far, ("rad", "az"), [(place, other ^ groups // 4) for place, other in turns])
    halo_phases, halo = pl.pallas_call(
        functools.partial(halo_kernel, groups=groups, rows=rows, blocks=blocks),
        out_shape=(float_of((2, half + rows, width)), float_of((QUAD, width))),
        in_specs=[SMEM] * 2 + [VMEM] * 2,
        out_specs=(VMEM,) * 2,
        compiler_params=PARAMS,
        cost_estimate=pl.CostEstimate(flops=10**8, transcendentals=10**4, bytes_accessed=2**18),
    )(column, block, near, far)
    pitch = rows + 1
    signal = pl.pallas_call(
        functools.partial(shear_kernel, groups=groups, rows=rows),
        out_shape=float_of((groups * pitch, width)),
        in_specs=[SMEM] + [VMEM] * 6,
        out_specs=VMEM,
        scratch_shapes=[pltpu.VMEM((2 * rows, width), jnp.float32)],
        compiler_params=PARAMS,
        cost_estimate=pl.CostEstimate(flops=10**9, transcendentals=0, bytes_accessed=2**21),
    )(column, signal.reshape(groups * rows, width), phases, halo, halo_phases, table, twist)
    signal = signal.reshape(groups, pitch, 1, width)
    signal = lax.all_to_all(signal, "az", 0, 0, axis_index_groups=[listed(BACK, groups)], tiled=True)
    signal = signal.reshape(groups * pitch, width)
    whole_shape = (sets, row_count, width)
    remapped, radial = pl.pallas_call(
        functools.partial(derivative_kernel, groups=groups, rows=rows),
        out_shape=(float_of(whole_shape), float_of(whole_shape)),
        in_specs=[VMEM] * 2,
        out_specs=(HBM, HBM),
        scratch_shapes=[
            pltpu.VMEM(whole_shape, jnp.float32),
            pltpu.VMEM(whole_shape, jnp.float32),
            pltpu.SemaphoreType.DMA((sets + sets * row_count // BLOCK,)),
        ],
        compiler_params=PARAMS,
    )(signal, matrix)
    return remapped.reshape(fields.shape), radial.reshape(fields.shape)


def solution(mesh):
    return jax.shard_map(
        on_device,
        mesh=mesh,
        in_specs=(P(None, None, "rad", "az"), P("rad"), P("rad"), P("rad")),
        out_specs=(P(None, None, "rad", "az"), P(None, None, "rad", "az")),
        check_vma=False,
    )
```
